32 devices in a mesh: pole: 2 (over y), row: 4 (over x, core), col: 4 (over z).
Axes of the slice: x: 2, y: 2, z: 4, core: 2. Of those that a mesh axis runs over, the one named last changes fastest.
Arguments:
- green_top: bfloat16 [4096, 2048], P(('pole', 'col'), 'row'), parts along dimension 0, may hold values from -6 to 6
- factor_cols: bfloat16 [1024, 2048], P(('pole', 'row', 'col')), parts along dimension 0, may hold values from -0.1875 to 0.1875
- fill_blocks: int32 [4, 8], replicated, may hold values from 0 to 1, as said below
- diag_inverse: float32 [1024, 128], P(('pole', 'row')), parts along dimension 0, may hold values from -6 to 6
Outputs:
- green_cols: float32 [1024, 2048], P(('pole', 'row'), 'col'), parts along dimension 0
- green_diag: float32 [1024, 128], P(('pole', 'row')), parts along dimension 0
The draws below stay inside these ranges and needn't reach their ends.
There are 2 independent parts, one for each index of `pole`. The reference program is written for one: setup_inputs(seed, part) draws one part's arguments, and reference() takes and returns one part's arrays. A program takes and returns all parts, laid end to end along the dimension named above; an argument that names none is the same for every part. Nothing has to cross between parts.
Inputs may be any that keep to these rules, and one draw needn't show every extreme that they name: `fill_blocks`: in every row, each aligned run of 8 // 4 blocks holds exactly half ones.
All inputs are finite; a program needn't handle non-finite values.
Results may differ from the reference program's by a relative error of at most 0.0003.
Values may be sent and summed in bfloat16 or wider, within the bound.
No kernel may reach another device: no remote copies, remote signals or barrier semaphores. Data moves between devices by JAX's collectives and lax.ppermute only.
A program may use at most 64 MiB of HBM per device.

```python
import jax
import jax.numpy as jnp
from jax import lax

SNODE = 128
BLOCK = 256
NTOP = 2048
NSUPER = 4
NCOLS = 512
NBLK = 8
N_COL = 4


def draw_fill_blocks(key, part):
    key = jax.random.fold_in(key, 7)
    group = NBLK // N_COL
    base = (jnp.arange(group) < group // 2).astype(jnp.int32)
    keys = jax.random.split(key, NSUPER * N_COL)
    runs = jax.vmap(lambda one_key: jax.random.permutation(one_key, base))(keys)
    return runs.reshape(NSUPER, NBLK).astype(jnp.int32)


def block_levels(own_key, dims, cuts, low, largest):
    factor_of = 1.0
    for position, parts in cuts:
        heights = jax.random.uniform(jax.random.fold_in(jax.random.fold_in(own_key, 6), position), (parts,), jnp.float32, low / len(cuts), largest / len(cuts))
        factor_of = factor_of * jnp.repeat(jnp.exp(heights), dims[position] // parts).reshape((-1,) + (1,) * (len(dims) - 1 - position))
    return factor_of


def centred(rng, dims, scale, most, shards=(), dtype=jnp.bfloat16):
    result = scale * jax.random.normal(rng, dims, jnp.float32)
    if shards:
        result = result * block_levels(rng, dims, shards, -0.22, 0.18)
    return jnp.clip(result, -most, most).astype(dtype)


def setup_inputs(seed: int = 0, part: int = 0) -> dict:
    splits = jax.random.split(jax.random.key(seed), 5)
    part_splits = jax.random.split(jax.random.fold_in(splits[4], part), 5)
    return {
        "green_top": centred(part_splits[0], (NTOP, NTOP), 1.0, 6.0, ((0, 4), (1, 4))),
        "factor_cols": centred(part_splits[1], (NCOLS, NTOP), (NTOP // 2) ** -0.5, 0.1875, ((0, 16),)),
        "fill_blocks": draw_fill_blocks(jax.random.fold_in(splits[4], 71), part),
        "diag_inverse": centred(part_splits[3], (NCOLS, SNODE), 1.0, 6.0, ((0, 4),), jnp.float32),
    }


def reference(green_top, factor_cols, fill_blocks, diag_inverse):
    fill = jnp.repeat(jnp.repeat(fill_blocks, SNODE, axis=0), BLOCK, axis=1)
    masked = factor_cols * fill.astype(jnp.bfloat16)
    solved = -lax.dot_general(masked, green_top, (((1,), (1,)), ((), ())), preferred_element_type=jnp.float32)
    green_cols = solved * fill.astype(jnp.float32)
    wide = masked.astype(jnp.float32).reshape(NSUPER, SNODE, NTOP)
    blocks = jnp.einsum("ksr,ktr->kst", solved.reshape(NSUPER, SNODE, NTOP), wide, precision=lax.Precision.HIGHEST)
    green_diag = diag_inverse - blocks.reshape(NSUPER * SNODE, SNODE)
    return green_cols, green_diag
```

```python
import jax
import jax.numpy as jnp
from jax import lax
from jax.sharding import PartitionSpec as P


def partner(value, axis, step):
    size = lax.axis_size(axis)
    return lax.ppermute(value, axis, [(a, a ^ step) for a in range(size)])


def filled(line, count):
    rank = jnp.cumsum(line) - 1
    place = jnp.arange(line.shape[0])
    return [jnp.sum(jnp.where((line == 1) & (rank == p), place, 0)) for p in range(count)]


def cut(value, rows, row_size, cols, col_size):
    return jnp.concatenate(
        [
            jnp.concatenate(
                [
                    lax.dynamic_slice(
                        value, (r * row_size, c * col_size), (row_size, col_size)
                    )
                    for c in cols
                ],
                axis=1,
            )
            for r in rows
        ],
        axis=0,
    )


def per_device(green_top, factor_cols, fill_blocks, diag_inverse):
    row_index = lax.axis_index("row")
    col_index = lax.axis_index("col")
    row_count = lax.axis_size("row")
    col_count = lax.axis_size("col")
    local_rows, order = factor_cols.shape
    blocks = fill_blocks.shape[1]
    size = order // blocks
    group = blocks // col_count
    half = group // 2
    chunk = blocks // row_count
    exact = chunk % group == 0
    kept = chunk // 2 if exact else chunk

    def fill_of(k, start, count):
        return lax.dynamic_slice(fill_blocks, (k, start), (1, count))[0]

    def chosen(k, part):
        if exact:
            return filled(fill_of(k, part * chunk, chunk), kept)
        return list(range(kept))

    fill_line = jnp.repeat(fill_of(row_index, 0, blocks), size)
    masked = factor_cols * fill_line.astype(jnp.bfloat16)[None, :]
    picks = [[part * chunk + b for b in chosen(row_index, part)] for part in range(row_count)]
    own_factor = jnp.concatenate(
        [
            lax.dynamic_slice(masked, (0, b * size), (local_rows, size))
            for pick in picks
            for b in pick
        ],
        axis=1,
    )
    factor_parts = {t: partner(own_factor, "col", t) for t in range(1, col_count)}
    factor_parts[0] = own_factor

    green_parts = {}
    for s in range(row_count):
        k = row_index ^ s
        rows = filled(fill_of(k, col_index * group, group), half)
        green_parts[s] = cut(green_top, rows, size, chosen(k, row_index), size)
    for s in range(1, row_count):
        green_parts[s] = partner(green_parts[s], "row", s)

    factor = jnp.zeros((col_count * local_rows, own_factor.shape[1]), jnp.bfloat16)
    for t in range(col_count):
        factor = lax.dynamic_update_slice(
            factor, factor_parts[t], ((col_index ^ t) * local_rows, 0)
        )
    width = kept * size
    solved = 0.0
    for s in range(row_count):
        part = lax.dynamic_slice(
            factor, (0, (row_index ^ s) * width), (factor.shape[0], width)
        )
        solved = solved - lax.dot_general(
            part, green_parts[s], (((1,), (1,)), ((), ())), preferred_element_type=jnp.float32
        )
    fill_own = fill_of(row_index, col_index * group, group)
    rows = filled(fill_own, half)
    if exact:
        places = [col_index * half + p for p in range(half)]
    else:
        places = [col_index * group + r for r in rows]
    factor_rows = jnp.concatenate(
        [
            lax.dynamic_slice(factor, (0, b * size), (factor.shape[0], size))
            for b in places
        ],
        axis=1,
    )
    partial_value = lax.dot_general(
        solved,
        factor_rows.astype(jnp.float32),
        (((1,), (1,)), ((), ())),
        precision=lax.Precision.HIGHEST,
        preferred_element_type=jnp.float32,
    )
    rank = jnp.cumsum(fill_own) - 1
    green_cols = jnp.concatenate(
        [
            sum(
                jnp.where((fill_own[b] == 1) & (rank[b] == p), 1.0, 0.0)
                * solved[:, p * size : (p + 1) * size]
                for p in range(half)
            )
            for b in range(group)
        ],
        axis=1,
    )
    sums = [partial_value] + [partner(partial_value, "col", t) for t in range(1, col_count)]
    while len(sums) > 1:
        sums = [a + b for a, b in zip(sums[::2], sums[1::2])]
    return (green_cols, diag_inverse - sums[0])


def solution(mesh):
    placed = (
        P(("pole", "col"), "row"),
        P(("pole", "row", "col"), None),
        P(),
        P(("pole", "row"), None),
    )
    return jax.shard_map(
        per_device,
        mesh=mesh,
        in_specs=placed,
        out_specs=(P(("pole", "row"), "col"), P(("pole", "row"), None)),
        check_vma=False,
    )
```

```python
import jax
import jax.numpy as jnp
from jax import lax
from jax.experimental import pallas as pl
from jax.experimental.pallas import tpu as pltpu
from jax.sharding import PartitionSpec as P


def partner(value, axis, step):
    size = lax.axis_size(axis)
    return lax.ppermute(value, axis, [(a, a ^ step) for a in range(size)])


def filled(line, count):
    rank = jnp.cumsum(line) - 1
    place = jnp.arange(line.shape[0])
    return [jnp.sum(jnp.where((line == 1) & (rank == p), place, 0)) for p in range(count)]


def cut(value, rows, row_size, cols, col_size):
    return jnp.concatenate(
        [
            jnp.concatenate(
                [
                    lax.dynamic_slice(
                        value, (r * row_size, c * col_size), (row_size, col_size)
                    )
                    for c in cols
                ],
                axis=1,
            )
            for r in rows
        ],
        axis=0,
    )


def wide_device(green_top, factor_cols, fill_blocks, diag_inverse):
    row_index = lax.axis_index("row")
    col_index = lax.axis_index("col")
    row_count = lax.axis_size("row")
    col_count = lax.axis_size("col")
    local_rows, order = factor_cols.shape
    blocks = fill_blocks.shape[1]
    size = order // blocks
    group = blocks // col_count
    half = group // 2
    chunk = blocks // row_count
    exact = chunk % group == 0
    kept = chunk // 2 if exact else chunk

    def fill_of(k, start, count):
        return lax.dynamic_slice(fill_blocks, (k, start), (1, count))[0]

    def chosen(k, part):
        if exact:
            return filled(fill_of(k, part * chunk, chunk), kept)
        return list(range(kept))

    fill_line = jnp.repeat(fill_of(row_index, 0, blocks), size)
    masked = factor_cols * fill_line.astype(jnp.bfloat16)[None, :]
    picks = [[part * chunk + b for b in chosen(row_index, part)] for part in range(row_count)]
    own_factor = jnp.concatenate(
        [
            lax.dynamic_slice(masked, (0, b * size), (local_rows, size))
            for pick in picks
            for b in pick
        ],
        axis=1,
    )
    factor_parts = {t: partner(own_factor, "col", t) for t in range(1, col_count)}
    factor_parts[0] = own_factor

    green_parts = {}
    for s in range(row_count):
        k = row_index ^ s
        rows = filled(fill_of(k, col_index * group, group), half)
        green_parts[s] = cut(green_top, rows, size, chosen(k, row_index), size)
    for s in range(1, row_count):
        green_parts[s] = partner(green_parts[s], "row", s)

    factor = jnp.zeros((col_count * local_rows, own_factor.shape[1]), jnp.bfloat16)
    for t in range(col_count):
        factor = lax.dynamic_update_slice(
            factor, factor_parts[t], ((col_index ^ t) * local_rows, 0)
        )
    width = kept * size
    solved = 0.0
    for s in range(row_count):
        part = lax.dynamic_slice(
            factor, (0, (row_index ^ s) * width), (factor.shape[0], width)
        )
        solved = solved - lax.dot_general(
            part, green_parts[s], (((1,), (1,)), ((), ())), preferred_element_type=jnp.float32
        )
    fill_own = fill_of(row_index, col_index * group, group)
    rows = filled(fill_own, half)
    if exact:
        places = [col_index * half + p for p in range(half)]
    else:
        places = [col_index * group + r for r in rows]
    factor_rows = jnp.concatenate(
        [
            lax.dynamic_slice(factor, (0, b * size), (factor.shape[0], size))
            for b in places
        ],
        axis=1,
    )
    partial_value = lax.dot_general(
        solved,
        factor_rows.astype(jnp.float32),
        (((1,), (1,)), ((), ())),
        precision=lax.Precision.HIGHEST,
        preferred_element_type=jnp.float32,
    )
    rank = jnp.cumsum(fill_own) - 1
    green_cols = jnp.concatenate(
        [
            sum(
                jnp.where((fill_own[b] == 1) & (rank[b] == p), 1.0, 0.0)
                * solved[:, p * size : (p + 1) * size]
                for p in range(half)
            )
            for b in range(group)
        ],
        axis=1,
    )
    sums = [partial_value] + [partner(partial_value, "col", t) for t in range(1, col_count)]
    while len(sums) > 1:
        sums = [a + b for a, b in zip(sums[::2], sums[1::2])]
    return (green_cols, diag_inverse - sums[0])


def pack_kernel(row_count, col_count, fill, green, factor, *refs):
    outs, sems = refs[:-1], refs[-1]
    own_factor, mask = outs[0], outs[1]
    greens = outs[2:]
    row_index = lax.axis_index("row")
    col_index = lax.axis_index("col")
    blocks = fill.shape[1]
    size = factor.shape[1] // blocks
    group = blocks // col_count
    half = group // 2
    chunk = blocks // row_count
    kept = chunk // 2

    def places(k, start, count, wanted):
        found = [0] * wanted
        rank = 0
        for b in range(count):
            one = fill[k, start + b]
            for p in range(wanted):
                found[p] = jnp.where((one == 1) & (rank == p), b, found[p])
            rank = rank + one
        return found

    copies = []

    def copy(source, target):
        one = pltpu.make_async_copy(source, target, sems.at[len(copies)])
        one.start()
        copies.append(one)

    for part in range(row_count):
        for p, b in enumerate(places(row_index, part * chunk, chunk, kept)):
            copy(
                factor.at[:, pl.ds(pl.multiple_of((part * chunk + b) * size, size), size)],
                own_factor.at[:, pl.ds((part * kept + p) * size, size)],
            )
    for s in range(row_count):
        k = row_index ^ s
        rows = places(k, col_index * group, group, half)
        cols = places(k, row_index * chunk, chunk, kept)
        for p, r in enumerate(rows):
            for q, c in enumerate(cols):
                copy(
                    green.at[
                        pl.ds(pl.multiple_of(r * size, size), size),
                        pl.ds(pl.multiple_of(c * size, size), size),
                    ],
                    greens[s].at[pl.ds(p * size, size), pl.ds(q * size, size)],
                )
        if s == 0:
            for p, r in enumerate(rows):
                for b in range(group):
                    mask[p : p + 1, b * size : (b + 1) * size] = jnp.full(
                        (1, size), jnp.where(r == b, 1.0, 0.0), jnp.float32
                    )
    for one in copies:
        one.wait()


def pack(green_top, factor_cols, fill_blocks):
    row_count = lax.axis_size("row")
    col_count = lax.axis_size("col")
    local_rows, order = factor_cols.shape
    blocks = fill_blocks.shape[1]
    size = order // blocks
    group = blocks // col_count
    half = group // 2
    kept = blocks // row_count // 2
    shapes = [
        pltpu.VMEM((local_rows, row_count * kept * size), jnp.bfloat16),
        pltpu.VMEM((half, group * size), jnp.float32),
    ] + [pltpu.VMEM((half * size, kept * size), jnp.bfloat16)] * row_count
    return pl.pallas_call(
        lambda *refs: pack_kernel(row_count, col_count, *refs),
        out_shape=shapes,
        in_specs=[
            pl.BlockSpec(memory_space=pltpu.SMEM),
            pl.BlockSpec(memory_space=pltpu.HBM),
            pl.BlockSpec(memory_space=pltpu.HBM),
        ],
        out_specs=[pl.BlockSpec(memory_space=pltpu.VMEM)] * len(shapes),
        scratch_shapes=[
            pltpu.SemaphoreType.DMA((row_count * kept + row_count * half * kept,))
        ],
        name="pack",
    )(fill_blocks, green_top, factor_cols)


def per_device(green_top, factor_cols, fill_blocks, diag_inverse):
    row_count = lax.axis_size("row")
    col_count = lax.axis_size("col")
    blocks = fill_blocks.shape[1]
    chunk = blocks // row_count
    group = blocks // col_count
    if chunk % group or green_top.size > 1 << 20:
        return wide_device(green_top, factor_cols, fill_blocks, diag_inverse)
    row_index = lax.axis_index("row")
    col_index = lax.axis_index("col")
    local_rows, order = factor_cols.shape
    size = order // blocks
    half = group // 2
    width = chunk // 2 * size

    own_factor, mask, *greens = pack(green_top, factor_cols, fill_blocks)
    factors = [own_factor] + [partner(own_factor, "col", t) for t in range(1, col_count)]
    greens = greens[:1] + [partner(greens[s], "row", s) for s in range(1, row_count)]
    factor = jnp.zeros((col_count * local_rows, own_factor.shape[1]), jnp.bfloat16)
    for t in range(col_count):
        factor = lax.dynamic_update_slice(
            factor, factors[t], ((col_index ^ t) * local_rows, 0)
        )
    solved = 0.0
    for s in range(row_count):
        part = lax.dynamic_slice(
            factor, (0, (row_index ^ s) * width), (factor.shape[0], width)
        )
        solved = solved - lax.dot_general(
            part, greens[s], (((1,), (1,)), ((), ())), preferred_element_type=jnp.float32
        )
    factor_rows = lax.dynamic_slice(
        factor, (0, col_index * half * size), (factor.shape[0], half * size)
    )
    partial_value = lax.dot_general(
        solved,
        factor_rows.astype(jnp.float32),
        (((1,), (1,)), ((), ())),
        precision=lax.Precision.HIGHEST,
        preferred_element_type=jnp.float32,
    )
    green_cols = sum(
        mask[p : p + 1] * jnp.tile(solved[:, p * size : (p + 1) * size], (1, group))
        for p in range(half)
    )
    sums = [partial_value] + [partner(partial_value, "col", t) for t in range(1, col_count)]
    while len(sums) > 1:
        sums = [a + b for a, b in zip(sums[::2], sums[1::2])]
    return (green_cols, diag_inverse - sums[0])


def solution(mesh):
    placed = (
        P(("pole", "col"), "row"),
        P(("pole", "row", "col"), None),
        P(),
        P(("pole", "row"), None),
    )
    return jax.shard_map(
        per_device,
        mesh=mesh,
        in_specs=placed,
        out_specs=(P(("pole", "row"), "col"), P(("pole", "row"), None)),
        check_vma=False,
    )
```

```python
import jax
import jax.numpy as jnp
from jax import lax
from jax.experimental import pallas as pl
from jax.experimental.pallas import tpu as pltpu
from jax.sharding import PartitionSpec as P


def partner(value, axis, step):
    size = lax.axis_size(axis)
    return lax.ppermute(value, axis, [(a, a ^ step) for a in range(size)])


def filled(line, count):
    rank = jnp.cumsum(line) - 1
    place = jnp.arange(line.shape[0])
    return [jnp.sum(jnp.where((line == 1) & (rank == p), place, 0)) for p in range(count)]


def cut(value, rows, row_size, cols, col_size):
    return jnp.concatenate(
        [
            jnp.concatenate(
                [
                    lax.dynamic_slice(
                        value, (r * row_size, c * col_size), (row_size, col_size)
                    )
                    for c in cols
                ],
                axis=1,
            )
            for r in rows
        ],
        axis=0,
    )


def wide_device(green_top, factor_cols, fill_blocks, diag_inverse):
    row_index = lax.axis_index("row")
    col_index = lax.axis_index("col")
    row_count = lax.axis_size("row")
    col_count = lax.axis_size("col")
    local_rows, order = factor_cols.shape
    blocks = fill_blocks.shape[1]
    size = order // blocks
    group = blocks // col_count
    half = group // 2
    chunk = blocks // row_count
    exact = chunk % group == 0
    kept = chunk // 2 if exact else chunk

    def fill_of(k, start, count):
        return lax.dynamic_slice(fill_blocks, (k, start), (1, count))[0]

    def chosen(k, part):
        if exact:
            return filled(fill_of(k, part * chunk, chunk), kept)
        return list(range(kept))

    fill_line = jnp.repeat(fill_of(row_index, 0, blocks), size)
    masked = factor_cols * fill_line.astype(jnp.bfloat16)[None, :]
    picks = [[part * chunk + b for b in chosen(row_index, part)] for part in range(row_count)]
    own_factor = jnp.concatenate(
        [
            lax.dynamic_slice(masked, (0, b * size), (local_rows, size))
            for pick in picks
            for b in pick
        ],
        axis=1,
    )
    factor_parts = {t: partner(own_factor, "col", t) for t in range(1, col_count)}
    factor_parts[0] = own_factor

    green_parts = {}
    for s in range(row_count):
        k = row_index ^ s
        rows = filled(fill_of(k, col_index * group, group), half)
        green_parts[s] = cut(green_top, rows, size, chosen(k, row_index), size)
    for s in range(1, row_count):
        green_parts[s] = partner(green_parts[s], "row", s)

    factor = jnp.zeros((col_count * local_rows, own_factor.shape[1]), jnp.bfloat16)
    for t in range(col_count):
        factor = lax.dynamic_update_slice(
            factor, factor_parts[t], ((col_index ^ t) * local_rows, 0)
        )
    width = kept * size
    solved = 0.0
    for s in range(row_count):
        part = lax.dynamic_slice(
            factor, (0, (row_index ^ s) * width), (factor.shape[0], width)
        )
        solved = solved - lax.dot_general(
            part, green_parts[s], (((1,), (1,)), ((), ())), preferred_element_type=jnp.float32
        )
    fill_own = fill_of(row_index, col_index * group, group)
    rows = filled(fill_own, half)
    if exact:
        places = [col_index * half + p for p in range(half)]
    else:
        places = [col_index * group + r for r in rows]
    factor_rows = jnp.concatenate(
        [
            lax.dynamic_slice(factor, (0, b * size), (factor.shape[0], size))
            for b in places
        ],
        axis=1,
    )
    partial_value = lax.dot_general(
        solved,
        factor_rows.astype(jnp.float32),
        (((1,), (1,)), ((), ())),
        precision=lax.Precision.HIGHEST,
        preferred_element_type=jnp.float32,
    )
    rank = jnp.cumsum(fill_own) - 1
    green_cols = jnp.concatenate(
        [
            sum(
                jnp.where((fill_own[b] == 1) & (rank[b] == p), 1.0, 0.0)
                * solved[:, p * size : (p + 1) * size]
                for p in range(half)
            )
            for b in range(group)
        ],
        axis=1,
    )
    sums = [partial_value] + [partner(partial_value, "col", t) for t in range(1, col_count)]
    while len(sums) > 1:
        sums = [a + b for a, b in zip(sums[::2], sums[1::2])]
    return (green_cols, diag_inverse - sums[0])


def places(fill, k, start, count, wanted):
    found = [0] * wanted
    rank = 0
    for b in range(count):
        one = fill[k, start + b]
        for p in range(wanted):
            found[p] = jnp.where((one == 1) & (rank == p), b, found[p])
        rank = rank + one
    return found


def block(at, size):
    return pl.ds(pl.multiple_of(at * size, size), size)


def pack_kernel(
    row_count, col_count, fill_in, green_in, factor_in, own_factor, mask, *refs
):
    greens, (fill, green, factor, sems) = refs[:row_count], refs[row_count:]
    copies = [
        pltpu.make_async_copy(source, target, sems.at[n])
        for n, (source, target) in enumerate(
            [(fill_in, fill), (factor_in, factor), (green_in, green)]
        )
    ]
    for one in copies:
        one.start()
    row_index = lax.axis_index("row")
    col_index = lax.axis_index("col")
    blocks = fill.shape[1]
    size = factor.shape[1] // blocks
    group = blocks // col_count
    half = group // 2
    chunk = blocks // row_count
    kept = chunk // 2
    copies[0].wait()
    chosen = [
        (
            places(fill, row_index ^ s, col_index * group, group, half),
            places(fill, row_index ^ s, row_index * chunk, chunk, kept),
        )
        for s in range(row_count)
    ]
    own = [
        part * chunk + b
        for part in range(row_count)
        for b in places(fill, row_index, part * chunk, chunk, kept)
    ]
    for p, r in enumerate(chosen[0][0]):
        for b in range(group):
            mask[p : p + 1, b * size : (b + 1) * size] = jnp.full(
                (1, size), jnp.where(r == b, 1.0, 0.0), jnp.float32
            )
    copies[1].wait()
    for p, b in enumerate(own):
        own_factor[:, p * size : (p + 1) * size] = factor[:, block(b, size)]
    copies[2].wait()
    for s, (rows, cols) in enumerate(chosen):
        for p, r in enumerate(rows):
            for q, c in enumerate(cols):
                greens[s][p * size : (p + 1) * size, q * size : (q + 1) * size] = green[
                    block(r, size), block(c, size)
                ]


def pack(green_top, factor_cols, fill_blocks):
    row_count = lax.axis_size("row")
    col_count = lax.axis_size("col")
    local_rows, order = factor_cols.shape
    blocks = fill_blocks.shape[1]
    size = order // blocks
    group = blocks // col_count
    half = group // 2
    kept = blocks // row_count // 2
    shapes = [
        pltpu.VMEM((local_rows, row_count * kept * size), jnp.bfloat16),
        pltpu.VMEM((half, group * size), jnp.float32),
    ] + [pltpu.VMEM((half * size, kept * size), jnp.bfloat16)] * row_count
    return pl.pallas_call(
        lambda *refs: pack_kernel(row_count, col_count, *refs),
        out_shape=shapes,
        in_specs=[pl.BlockSpec(memory_space=pltpu.HBM)] * 3,
        out_specs=[pl.BlockSpec(memory_space=pltpu.VMEM)] * len(shapes),
        scratch_shapes=[
            pltpu.SMEM(fill_blocks.shape, fill_blocks.dtype),
            pltpu.VMEM(green_top.shape, green_top.dtype),
            pltpu.VMEM(factor_cols.shape, factor_cols.dtype),
            pltpu.SemaphoreType.DMA((3,)),
        ],
        name="pack",
    )(fill_blocks, green_top, factor_cols)


def solve_kernel(row_count, col_count, *refs):
    factors, refs = refs[:col_count], refs[col_count:]
    greens, (solved, partial_value, factor) = refs[:row_count], refs[row_count:]
    row_index = lax.axis_index("row")
    col_index = lax.axis_index("col")
    local_rows = factors[0].shape[0]
    rows, width = greens[0].shape
    for t in range(col_count):
        factor[block(col_index ^ t, local_rows), :] = factors[t][...]
    total = jnp.zeros(solved.shape, jnp.float32)
    for s in range(row_count):
        total = total + lax.dot_general(
            factor[:, block(row_index ^ s, width)],
            greens[s][...],
            (((1,), (1,)), ((), ())),
            preferred_element_type=jnp.float32,
        )
    total = -total
    solved[...] = total
    pieces = []
    rest = total
    for _ in range(3):
        pieces.append(rest.astype(jnp.bfloat16))
        rest = rest - pieces[-1].astype(jnp.float32)
    own = factor[:, block(col_index, rows)]
    value = 0.0
    for piece in pieces[::-1]:
        value = value + lax.dot_general(
            piece, own, (((1,), (1,)), ((), ())), preferred_element_type=jnp.float32
        )
    partial_value[...] = value


def solve(factors, greens):
    col_count, row_count = len(factors), len(greens)
    local_rows, columns = factors[0].shape
    count = col_count * local_rows
    return pl.pallas_call(
        lambda *refs: solve_kernel(row_count, col_count, *refs),
        out_shape=[
            pltpu.VMEM((count, greens[0].shape[0]), jnp.float32),
            pltpu.VMEM((count, count), jnp.float32),
        ],
        in_specs=[pl.BlockSpec(memory_space=pltpu.VMEM)] * (row_count + col_count),
        out_specs=[pl.BlockSpec(memory_space=pltpu.VMEM)] * 2,
        scratch_shapes=[pltpu.VMEM((count, columns), jnp.bfloat16)],
        compiler_params=pltpu.CompilerParams(vmem_limit_bytes=32 * 1024 * 1024),
        name="solve",
    )(*factors, *greens)


def per_device(green_top, factor_cols, fill_blocks, diag_inverse):
    row_count = lax.axis_size("row")
    col_count = lax.axis_size("col")
    blocks = fill_blocks.shape[1]
    chunk = blocks // row_count
    group = blocks // col_count
    if chunk % group or green_top.size > 1 << 20:
        return wide_device(green_top, factor_cols, fill_blocks, diag_inverse)
    half = group // 2
    size = factor_cols.shape[1] // blocks

    own_factor, mask, *greens = pack(green_top, factor_cols, fill_blocks)
    factors = [own_factor] + [partner(own_factor, "col", t) for t in range(1, col_count)]
    greens = greens[:1] + [partner(greens[s], "row", s) for s in range(1, row_count)]
    solved, partial_value = solve(factors, greens)
    green_cols = None
    for p in range(half):
        term = mask[p : p + 1] * jnp.tile(solved[:, p * size : (p + 1) * size], (1, group))
        green_cols = term if green_cols is None else green_cols + term
    sums = [partial_value] + [partner(partial_value, "col", t) for t in range(1, col_count)]
    while len(sums) > 1:
        sums = [a + b for a, b in zip(sums[::2], sums[1::2])]
    return (green_cols, diag_inverse - sums[0])


def solution(mesh):
    placed = (
        P(("pole", "col"), "row"),
        P(("pole", "row", "col"), None),
        P(),
        P(("pole", "row"), None),
    )
    return jax.shard_map(
        per_device,
        mesh=mesh,
        in_specs=placed,
        out_specs=(P(("pole", "row"), "col"), P(("pole", "row"), None)),
        check_vma=False,
    )
```

```python
import jax
import jax.numpy as jnp
from jax import lax
from jax.experimental import pallas as pl
from jax.experimental.pallas import tpu as pltpu
from jax.sharding import PartitionSpec as P


EXPONENT_ROWS = 16
OPERANDS = (0, 4, 6, 7, 2, 1, 5, 3)


def partner(value, axis, step):
    size = lax.axis_size(axis)
    return lax.ppermute(value, axis, [(a, a ^ step) for a in range(size)])


def filled(line, count):
    rank = jnp.cumsum(line) - 1
    place = jnp.arange(line.shape[0])
    return [jnp.sum(jnp.where((line == 1) & (rank == p), place, 0)) for p in range(count)]


def cut(value, rows, row_size, cols, col_size):
    return jnp.concatenate(
        [
            jnp.concatenate(
                [
                    lax.dynamic_slice(
                        value, (r * row_size, c * col_size), (row_size, col_size)
                    )
                    for c in cols
                ],
                axis=1,
            )
            for r in rows
        ],
        axis=0,
    )


def wide_device(green_top, factor_cols, fill_blocks, diag_inverse):
    row_index = lax.axis_index("row")
    col_index = lax.axis_index("col")
    row_count = lax.axis_size("row")
    col_count = lax.axis_size("col")
    local_rows, order = factor_cols.shape
    blocks = fill_blocks.shape[1]
    size = order // blocks
    group = blocks // col_count
    half = group // 2
    chunk = blocks // row_count
    exact = chunk % group == 0
    kept = chunk // 2 if exact else chunk

    def fill_of(k, start, count):
        return lax.dynamic_slice(fill_blocks, (k, start), (1, count))[0]

    def chosen(k, part):
        if exact:
            return filled(fill_of(k, part * chunk, chunk), kept)
        return list(range(kept))

    fill_line = jnp.repeat(fill_of(row_index, 0, blocks), size)
    masked = factor_cols * fill_line.astype(jnp.bfloat16)[None, :]
    picks = [[part * chunk + b for b in chosen(row_index, part)] for part in range(row_count)]
    own_factor = jnp.concatenate(
        [
            lax.dynamic_slice(masked, (0, b * size), (local_rows, size))
            for pick in picks
            for b in pick
        ],
        axis=1,
    )
    factor_parts = {t: partner(own_factor, "col", t) for t in range(1, col_count)}
    factor_parts[0] = own_factor

    green_parts = {}
    for s in range(row_count):
        k = row_index ^ s
        rows = filled(fill_of(k, col_index * group, group), half)
        green_parts[s] = cut(green_top, rows, size, chosen(k, row_index), size)
    for s in range(1, row_count):
        green_parts[s] = partner(green_parts[s], "row", s)

    factor = jnp.zeros((col_count * local_rows, own_factor.shape[1]), jnp.bfloat16)
    for t in range(col_count):
        factor = lax.dynamic_update_slice(
            factor, factor_parts[t], ((col_index ^ t) * local_rows, 0)
        )
    width = kept * size
    solved = 0.0
    for s in range(row_count):
        part = lax.dynamic_slice(
            factor, (0, (row_index ^ s) * width), (factor.shape[0], width)
        )
        solved = solved - lax.dot_general(
            part, green_parts[s], (((1,), (1,)), ((), ())), preferred_element_type=jnp.float32
        )
    fill_own = fill_of(row_index, col_index * group, group)
    rows = filled(fill_own, half)
    if exact:
        places = [col_index * half + p for p in range(half)]
    else:
        places = [col_index * group + r for r in rows]
    factor_rows = jnp.concatenate(
        [
            lax.dynamic_slice(factor, (0, b * size), (factor.shape[0], size))
            for b in places
        ],
        axis=1,
    )
    partial_value = lax.dot_general(
        solved,
        factor_rows.astype(jnp.float32),
        (((1,), (1,)), ((), ())),
        precision=lax.Precision.HIGHEST,
        preferred_element_type=jnp.float32,
    )
    rank = jnp.cumsum(fill_own) - 1
    green_cols = jnp.concatenate(
        [
            sum(
                jnp.where((fill_own[b] == 1) & (rank[b] == p), 1.0, 0.0)
                * solved[:, p * size : (p + 1) * size]
                for p in range(half)
            )
            for b in range(group)
        ],
        axis=1,
    )
    sums = [partial_value] + [partner(partial_value, "col", t) for t in range(1, col_count)]
    while len(sums) > 1:
        sums = [a + b for a, b in zip(sums[::2], sums[1::2])]
    return (green_cols, diag_inverse - sums[0])


def places(fill, k, start, count, wanted):
    found = [0] * wanted
    rank = 0
    for b in range(count):
        one = fill[k, start + b]
        for p in range(wanted):
            found[p] = jnp.where((one == 1) & (rank == p), b, found[p])
        rank = rank + one
    return found


def block(at, size):
    return pl.ds(pl.multiple_of(at * size, size), size)


def pack_kernel(
    row_count, col_count, fill_in, green_in, factor_in, own_factor, mask, *refs
):
    greens, (fill, green, factor, sems) = refs[:row_count], refs[row_count:]
    copies = [
        pltpu.make_async_copy(source, target, sems.at[n])
        for n, (source, target) in enumerate(
            [(fill_in, fill), (factor_in, factor), (green_in, green)]
        )
    ]
    for one in copies:
        one.start()
    row_index = lax.axis_index("row")
    col_index = lax.axis_index("col")
    blocks = fill.shape[1]
    size = factor.shape[1] // blocks
    group = blocks // col_count
    half = group // 2
    chunk = blocks // row_count
    kept = chunk // 2
    copies[0].wait()
    chosen = [
        (
            places(fill, row_index ^ s, col_index * group, group, half),
            places(fill, row_index ^ s, row_index * chunk, chunk, kept),
        )
        for s in range(row_count)
    ]
    own = [
        part * chunk + b
        for part in range(row_count)
        for b in places(fill, row_index, part * chunk, chunk, kept)
    ]
    for p, r in enumerate(chosen[0][0]):
        for b in range(group):
            mask[p : p + 1, b * size : (b + 1) * size] = jnp.full(
                (1, size), jnp.where(r == b, 1.0, 0.0), jnp.float32
            )
    copies[1].wait()
    for p, b in enumerate(own):
        own_factor[:, p * size : (p + 1) * size] = factor[:, block(b, size)]
    copies[2].wait()
    for s, (rows, cols) in enumerate(chosen):
        for p, r in enumerate(rows):
            for q, c in enumerate(cols):
                greens[s][p * size : (p + 1) * size, q * size : (q + 1) * size] = green[
                    block(r, size), block(c, size)
                ]


def pack(green_top, factor_cols, fill_blocks):
    row_count = lax.axis_size("row")
    col_count = lax.axis_size("col")
    local_rows, order = factor_cols.shape
    blocks = fill_blocks.shape[1]
    size = order // blocks
    group = blocks // col_count
    half = group // 2
    kept = blocks // row_count // 2
    shapes = [
        pltpu.VMEM((local_rows, row_count * kept * size), jnp.bfloat16),
        pltpu.VMEM((half, group * size), jnp.float32),
    ] + [pltpu.VMEM((half * size, kept * size), jnp.bfloat16)] * row_count
    return pl.pallas_call(
        lambda *refs: pack_kernel(row_count, col_count, *refs),
        out_shape=shapes,
        in_specs=[pl.BlockSpec(memory_space=pltpu.HBM)] * 3,
        out_specs=[pl.BlockSpec(memory_space=pltpu.VMEM)] * len(shapes),
        scratch_shapes=[
            pltpu.SMEM(fill_blocks.shape, fill_blocks.dtype),
            pltpu.VMEM(green_top.shape, green_top.dtype),
            pltpu.VMEM(factor_cols.shape, factor_cols.dtype),
            pltpu.SemaphoreType.DMA((3,)),
        ],
        name="pack",
    )(fill_blocks, green_top, factor_cols)


def split(given, row_count, col_count):
    order = OPERANDS if (row_count, col_count) == (4, 4) else range(row_count + col_count)
    placed = dict(zip(order, given))
    return [placed[n] for n in range(col_count)], [
        placed[col_count + n] for n in range(row_count)
    ]


def solve_kernel(row_count, col_count, *refs):
    given, (solved, coded, factor) = refs[: row_count + col_count], refs[row_count + col_count :]
    factors, greens = split(given, row_count, col_count)
    row_index = lax.axis_index("row")
    col_index = lax.axis_index("col")
    local_rows = factors[0].shape[0]
    rows, width = greens[0].shape
    for t in range(col_count):
        factor[block(col_index ^ t, local_rows), :] = factors[t][...]
    total = jnp.zeros(solved.shape, jnp.float32)
    for s in range(row_count):
        total = total + lax.dot_general(
            factor[:, block(row_index ^ s, width)],
            greens[s][...],
            (((1,), (1,)), ((), ())),
            preferred_element_type=jnp.float32,
        )
    total = -total
    solved[...] = total
    pieces = []
    rest = total
    for _ in range(3):
        pieces.append(rest.astype(jnp.bfloat16))
        rest = rest - pieces[-1].astype(jnp.float32)
    own = factor[:, block(col_index, rows)]
    value = 0.0
    for piece in pieces[::-1]:
        value = value + lax.dot_general(
            piece, own, (((1,), (1,)), ((), ())), preferred_element_type=jnp.float32
        )
    largest = jnp.max(jnp.abs(value), axis=0, keepdims=True)
    exponent = jnp.floor(jnp.log2(jnp.maximum(largest, 2.0**-100)))
    scaled = jnp.round(value * jnp.exp2(14.0 - exponent))
    count = value.shape[0]
    coded[:count, :] = jnp.clip(scaled, -32767.0, 32767.0).astype(jnp.int32).astype(jnp.int16)
    coded[count:, :] = jnp.broadcast_to(
        exponent.astype(jnp.int32), (EXPONENT_ROWS, value.shape[1])
    ).astype(jnp.int16)


def solve(factors, greens):
    col_count, row_count = len(factors), len(greens)
    local_rows, columns = factors[0].shape
    count = col_count * local_rows
    return pl.pallas_call(
        lambda *refs: solve_kernel(row_count, col_count, *refs),
        out_shape=[
            pltpu.VMEM((count, greens[0].shape[0]), jnp.float32),
            pltpu.VMEM((count + EXPONENT_ROWS, count), jnp.int16),
        ],
        in_specs=[pl.BlockSpec(memory_space=pltpu.VMEM)] * (row_count + col_count),
        out_specs=[pl.BlockSpec(memory_space=pltpu.VMEM)] * 2,
        scratch_shapes=[pltpu.VMEM((count, columns), jnp.bfloat16)],
        compiler_params=pltpu.CompilerParams(vmem_limit_bytes=32 * 1024 * 1024),
        name="solve",
    )(*[(list(factors) + list(greens))[n] for n in (OPERANDS if (row_count, col_count) == (4, 4) else range(row_count + col_count))])


def finish_kernel(diag_inverse, *refs):
    codes, out = refs[:-1], refs[-1]
    count = diag_inverse.shape[0]
    sums = []
    for code in codes:
        exponent = code[count:, :].astype(jnp.int32).astype(jnp.float32)[:1]
        sums.append(code[:count, :].astype(jnp.int32).astype(jnp.float32) * jnp.exp2(exponent - 14.0))
    sums = [sums[n] for n in [0, 1, 3, 2]]
    while len(sums) > 1:
        sums = [a + b for a, b in zip(sums[::2], sums[1::2])]
    out[...] = diag_inverse[...] - sums[0]


def finish(diag_inverse, codes):
    return pl.pallas_call(
        finish_kernel,
        out_shape=jax.ShapeDtypeStruct(diag_inverse.shape, diag_inverse.dtype),
        in_specs=[pl.BlockSpec(memory_space=pltpu.VMEM)] * (1 + len(codes)),
        out_specs=pl.BlockSpec(memory_space=pltpu.VMEM),
        compiler_params=pltpu.CompilerParams(vmem_limit_bytes=32 * 1024 * 1024),
        name="finish",
    )(diag_inverse, *codes)


def per_device(green_top, factor_cols, fill_blocks, diag_inverse):
    row_count = lax.axis_size("row")
    col_count = lax.axis_size("col")
    blocks = fill_blocks.shape[1]
    chunk = blocks // row_count
    group = blocks // col_count
    if chunk % group or green_top.size > 1 << 20:
        return wide_device(green_top, factor_cols, fill_blocks, diag_inverse)
    half = group // 2
    size = factor_cols.shape[1] // blocks

    own_factor, mask, *greens = pack(green_top, factor_cols, fill_blocks)
    far, cross = partner(greens[2], "row", 2), partner(greens[3], "row", 3)
    near = partner(greens[1], "row", 1)
    parts = {"c": near, "x": far, "xc": cross}
    parts["z2"] = partner(own_factor, "col", 2)
    parts["z1"] = partner(own_factor, "col", 1)
    held = []
    passed, *rest = lax.optimization_barrier((parts["z2"], *[parts[n] for n in held]))
    parts.update(zip(held, rest))
    parts["z3"] = partner(passed, "col", 1)
    greens = [greens[0], parts["c"], parts["x"], parts["xc"]]
    factors = [own_factor] + [parts["z%d" % t] for t in range(1, col_count)]
    solved, code = solve(factors, greens)
    green_cols = None
    for p in range(half):
        term = mask[p : p + 1] * jnp.tile(solved[:, p * size : (p + 1) * size], (1, group))
        green_cols = term if green_cols is None else green_cols + term
    codes = [code] + [partner(code, "col", t) for t in [1, 3, 2]]
    return (green_cols, finish(diag_inverse, codes))


def solution(mesh):
    placed = (
        P(("pole", "col"), "row"),
        P(("pole", "row", "col"), None),
        P(),
        P(("pole", "row"), None),
    )
    return jax.shard_map(
        per_device,
        mesh=mesh,
        in_specs=placed,
        out_specs=(P(("pole", "row"), "col"), P(("pole", "row"), None)),
        check_vma=False,
    )
```

```python
import jax
import jax.numpy as jnp
from jax import lax
from jax.experimental import pallas as pl
from jax.experimental.pallas import tpu as pltpu
from jax.sharding import PartitionSpec as P


EXPONENT_ROWS = 16
RING = (1, 3, 0, 2)
BACK = (2, 0, 3, 1)
ACROSS = (3, 2, 1, 0)
VMEM_LIMIT = 32 * 1024 * 1024


def partner(value, axis, step):
    size = lax.axis_size(axis)
    return lax.ppermute(value, axis, [(a, a ^ step) for a in range(size)])


def filled(line, count):
    rank = jnp.cumsum(line) - 1
    place = jnp.arange(line.shape[0])
    return [jnp.sum(jnp.where((line == 1) & (rank == p), place, 0)) for p in range(count)]


def cut(value, rows, row_size, cols, col_size):
    return jnp.concatenate(
        [
            jnp.concatenate(
                [
                    lax.dynamic_slice(
                        value, (r * row_size, c * col_size), (row_size, col_size)
                    )
                    for c in cols
                ],
                axis=1,
            )
            for r in rows
        ],
        axis=0,
    )


def wide_device(green_top, factor_cols, fill_blocks, diag_inverse):
    row_index = lax.axis_index("row")
    col_index = lax.axis_index("col")
    row_count = lax.axis_size("row")
    col_count = lax.axis_size("col")
    local_rows, order = factor_cols.shape
    blocks = fill_blocks.shape[1]
    size = order // blocks
    group = blocks // col_count
    half = group // 2
    chunk = blocks // row_count
    exact = chunk % group == 0
    kept = chunk // 2 if exact else chunk

    def fill_of(k, start, count):
        return lax.dynamic_slice(fill_blocks, (k, start), (1, count))[0]

    def chosen(k, part):
        if exact:
            return filled(fill_of(k, part * chunk, chunk), kept)
        return list(range(kept))

    fill_line = jnp.repeat(fill_of(row_index, 0, blocks), size)
    masked = factor_cols * fill_line.astype(jnp.bfloat16)[None, :]
    picks = [[part * chunk + b for b in chosen(row_index, part)] for part in range(row_count)]
    own_factor = jnp.concatenate(
        [
            lax.dynamic_slice(masked, (0, b * size), (local_rows, size))
            for pick in picks
            for b in pick
        ],
        axis=1,
    )
    factor_parts = {t: partner(own_factor, "col", t) for t in range(1, col_count)}
    factor_parts[0] = own_factor

    green_parts = {}
    for s in range(row_count):
        k = row_index ^ s
        rows = filled(fill_of(k, col_index * group, group), half)
        green_parts[s] = cut(green_top, rows, size, chosen(k, row_index), size)
    for s in range(1, row_count):
        green_parts[s] = partner(green_parts[s], "row", s)

    factor = jnp.zeros((col_count * local_rows, own_factor.shape[1]), jnp.bfloat16)
    for t in range(col_count):
        factor = lax.dynamic_update_slice(
            factor, factor_parts[t], ((col_index ^ t) * local_rows, 0)
        )
    width = kept * size
    solved = 0.0
    for s in range(row_count):
        part = lax.dynamic_slice(
            factor, (0, (row_index ^ s) * width), (factor.shape[0], width)
        )
        solved = solved - lax.dot_general(
            part, green_parts[s], (((1,), (1,)), ((), ())), preferred_element_type=jnp.float32
        )
    fill_own = fill_of(row_index, col_index * group, group)
    rows = filled(fill_own, half)
    if exact:
        places = [col_index * half + p for p in range(half)]
    else:
        places = [col_index * group + r for r in rows]
    factor_rows = jnp.concatenate(
        [
            lax.dynamic_slice(factor, (0, b * size), (factor.shape[0], size))
            for b in places
        ],
        axis=1,
    )
    partial_value = lax.dot_general(
        solved,
        factor_rows.astype(jnp.float32),
        (((1,), (1,)), ((), ())),
        precision=lax.Precision.HIGHEST,
        preferred_element_type=jnp.float32,
    )
    rank = jnp.cumsum(fill_own) - 1
    green_cols = jnp.concatenate(
        [
            sum(
                jnp.where((fill_own[b] == 1) & (rank[b] == p), 1.0, 0.0)
                * solved[:, p * size : (p + 1) * size]
                for p in range(half)
            )
            for b in range(group)
        ],
        axis=1,
    )
    sums = [partial_value] + [partner(partial_value, "col", t) for t in range(1, col_count)]
    while len(sums) > 1:
        sums = [a + b for a, b in zip(sums[::2], sums[1::2])]
    return (green_cols, diag_inverse - sums[0])


def places(fill, k, start, count, wanted):
    found = [0] * wanted
    rank = 0
    for b in range(count):
        one = fill[k, start + b]
        for p in range(wanted):
            found[p] = jnp.where((one == 1) & (rank == p), b, found[p])
        rank = rank + one
    return found


def block(at, size):
    return pl.ds(pl.multiple_of(at * size, size), size)


def pack_kernel(
    row_count, col_count, fill_in, green_in, factor_in, own_factor, mask, *refs
):
    greens, (fill, green, factor, sems) = refs[:row_count], refs[row_count:]
    copies = [
        pltpu.make_async_copy(source, target, sems.at[n])
        for n, (source, target) in enumerate(
            [(fill_in, fill), (factor_in, factor), (green_in, green)]
        )
    ]
    for one in copies:
        one.start()
    row_index = lax.axis_index("row")
    col_index = lax.axis_index("col")
    blocks = fill.shape[1]
    size = factor.shape[1] // blocks
    group = blocks // col_count
    half = group // 2
    chunk = blocks // row_count
    kept = chunk // 2
    copies[0].wait()
    chosen = [
        (
            places(fill, row_index ^ s, col_index * group, group, half),
            places(fill, row_index ^ s, row_index * chunk, chunk, kept),
        )
        for s in range(row_count)
    ]
    own = [
        part * chunk + b
        for part in range(row_count)
        for b in places(fill, row_index, part * chunk, chunk, kept)
    ]
    for p, r in enumerate(chosen[0][0]):
        for b in range(group):
            mask[p : p + 1, b * size : (b + 1) * size] = jnp.full(
                (1, size), jnp.where(r == b, 1.0, 0.0), jnp.float32
            )
    copies[1].wait()
    for p, b in enumerate(own):
        own_factor[:, p * size : (p + 1) * size] = factor[:, block(b, size)]
    copies[2].wait()
    for s, (rows, cols) in enumerate(chosen):
        for p, r in enumerate(rows):
            for q, c in enumerate(cols):
                greens[s][p * size : (p + 1) * size, q * size : (q + 1) * size] = green[
                    block(r, size), block(c, size)
                ]


def pack(green_top, factor_cols, fill_blocks):
    row_count = lax.axis_size("row")
    col_count = lax.axis_size("col")
    local_rows, order = factor_cols.shape
    blocks = fill_blocks.shape[1]
    size = order // blocks
    group = blocks // col_count
    half = group // 2
    kept = blocks // row_count // 2
    shapes = [
        pltpu.VMEM((local_rows, row_count * kept * size), jnp.bfloat16),
        pltpu.VMEM((half, group * size), jnp.float32),
    ] + [pltpu.VMEM((half * size, kept * size), jnp.bfloat16)] * row_count
    return pl.pallas_call(
        lambda *refs: pack_kernel(row_count, col_count, *refs),
        out_shape=shapes,
        in_specs=[pl.BlockSpec(memory_space=pltpu.HBM)] * 3,
        out_specs=[pl.BlockSpec(memory_space=pltpu.VMEM)] * len(shapes),
        scratch_shapes=[
            pltpu.SMEM(fill_blocks.shape, fill_blocks.dtype),
            pltpu.VMEM(green_top.shape, green_top.dtype),
            pltpu.VMEM(factor_cols.shape, factor_cols.dtype),
            pltpu.SemaphoreType.DMA((3,)),
        ],
        name="pack",
    )(fill_blocks, green_top, factor_cols)


def code_of(value, coded):
    largest = jnp.max(jnp.abs(value), axis=0, keepdims=True)
    exponent = jnp.floor(jnp.log2(jnp.maximum(largest, 2.0**-100)))
    scaled = jnp.round(value * jnp.exp2(14.0 - exponent))
    count = value.shape[0]
    coded[:count, :] = jnp.clip(scaled, -32767.0, 32767.0).astype(jnp.int32).astype(jnp.int16)
    coded[count:, :] = jnp.broadcast_to(
        exponent.astype(jnp.int32), (EXPONENT_ROWS, value.shape[1])
    ).astype(jnp.int16)


def value_of(coded):
    count = coded.shape[0] - EXPONENT_ROWS
    exponent = coded[count:, :].astype(jnp.int32).astype(jnp.float32)[:1]
    return coded[:count, :].astype(jnp.int32).astype(jnp.float32) * jnp.exp2(exponent - 14.0)


def solve_kernel(origins, own_factor, own_green, *refs):
    given, (solved, coded, factor) = refs[:-3], refs[-3:]
    row_index = lax.axis_index("row")
    col_index = lax.axis_index("col")
    local_rows = own_factor.shape[0]
    rows, width = own_green.shape
    greens = [(0, own_green)]
    factor[block(col_index, local_rows), :] = own_factor[...]
    for (axis, step), part in zip(origins, given):
        if axis == "col":
            factor[block(col_index ^ step, local_rows), :] = part[...]
        else:
            greens.append((step, part))
    total = jnp.zeros(solved.shape, jnp.float32)
    for step, green in sorted(greens, key=lambda one: one[0]):
        total = total + lax.dot_general(
            factor[:, block(row_index ^ step, width)],
            green[...],
            (((1,), (1,)), ((), ())),
            preferred_element_type=jnp.float32,
        )
    total = -total
    solved[...] = total
    pieces = []
    rest = total
    for _ in range(3):
        pieces.append(rest.astype(jnp.bfloat16))
        rest = rest - pieces[-1].astype(jnp.float32)
    own = factor[:, block(col_index, rows)]
    value = 0.0
    for piece in pieces[::-1]:
        value = value + lax.dot_general(
            piece, own, (((1,), (1,)), ((), ())), preferred_element_type=jnp.float32
        )
    code_of(value, coded)


def solve(own_factor, own_green, origins, given, col_count):
    local_rows, columns = own_factor.shape
    count = col_count * local_rows
    return pl.pallas_call(
        lambda *refs: solve_kernel(origins, *refs),
        out_shape=[
            pltpu.VMEM((count, own_green.shape[0]), jnp.float32),
            pltpu.VMEM((count + EXPONENT_ROWS, count), jnp.int16),
        ],
        in_specs=[pl.BlockSpec(memory_space=pltpu.VMEM)] * (2 + len(given)),
        out_specs=[pl.BlockSpec(memory_space=pltpu.VMEM)] * 2,
        scratch_shapes=[pltpu.VMEM((count, columns), jnp.bfloat16)],
        compiler_params=pltpu.CompilerParams(vmem_limit_bytes=VMEM_LIMIT),
        name="solve",
    )(own_factor, own_green, *given)


def finish_kernel(diag_inverse, own, back, across, ring, out):
    total = (value_of(own) + value_of(across)) + (value_of(ring) + value_of(back))
    out[...] = diag_inverse[...] - total


def finish(diag_inverse, codes):
    return pl.pallas_call(
        finish_kernel,
        out_shape=jax.ShapeDtypeStruct(diag_inverse.shape, diag_inverse.dtype),
        in_specs=[pl.BlockSpec(memory_space=pltpu.VMEM)] * (1 + len(codes)),
        out_specs=pl.BlockSpec(memory_space=pltpu.VMEM),
        compiler_params=pltpu.CompilerParams(vmem_limit_bytes=VMEM_LIMIT),
        name="finish",
    )(diag_inverse, *codes)


def per_device(green_top, factor_cols, fill_blocks, diag_inverse):
    row_count = lax.axis_size("row")
    col_count = lax.axis_size("col")
    blocks = fill_blocks.shape[1]
    chunk = blocks // row_count
    group = blocks // col_count
    fits = row_count == 4 and col_count == 4 and chunk % group == 0
    if not fits or green_top.size > 1 << 20:
        return wide_device(green_top, factor_cols, fill_blocks, diag_inverse)
    half = group // 2
    size = factor_cols.shape[1] // blocks

    own_factor, mask, *greens = pack(green_top, factor_cols, fill_blocks)
    second = partner(own_factor, "col", 2)
    received = {
        ("row", 2): partner(greens[2], "row", 2),
        ("row", 3): partner(greens[3], "row", 3),
        ("row", 1): partner(greens[1], "row", 1),
        ("col", 2): second,
        ("col", 1): partner(own_factor, "col", 1),
        ("col", 3): partner(second, "col", 1),
    }
    solved, code = solve(
        own_factor, greens[0], tuple(received), tuple(received.values()), col_count
    )
    green_cols = None
    for p in range(half):
        term = mask[p : p + 1] * jnp.tile(solved[:, p * size : (p + 1) * size], (1, group))
        green_cols = term if green_cols is None else green_cols + term
    codes = [code] + [
        lax.ppermute(code, "col", list(enumerate(moves))) for moves in (BACK, ACROSS, RING)
    ]
    return (green_cols, finish(diag_inverse, codes))


def solution(mesh):
    placed = (
        P(("pole", "col"), "row"),
        P(("pole", "row", "col"), None),
        P(),
        P(("pole", "row"), None),
    )
    return jax.shard_map(
        per_device,
        mesh=mesh,
        in_specs=placed,
        out_specs=(P(("pole", "row"), "col"), P(("pole", "row"), None)),
        check_vma=False,
    )
```

```python
import jax
import jax.numpy as jnp
from jax import lax
from jax.experimental import pallas as pl
from jax.experimental.pallas import tpu as pltpu
from jax.sharding import PartitionSpec as P


EXPONENT_ROWS = 16
RING = (1, 3, 0, 2)
BACK = (2, 0, 3, 1)
ACROSS = (3, 2, 1, 0)
VMEM_LIMIT = 32 * 1024 * 1024


def partner(value, axis, step):
    size = lax.axis_size(axis)
    return lax.ppermute(value, axis, [(a, a ^ step) for a in range(size)])


def filled(line, count):
    rank = jnp.cumsum(line) - 1
    place = jnp.arange(line.shape[0])
    return [jnp.sum(jnp.where((line == 1) & (rank == p), place, 0)) for p in range(count)]


def cut(value, rows, row_size, cols, col_size):
    return jnp.concatenate(
        [
            jnp.concatenate(
                [
                    lax.dynamic_slice(
                        value, (r * row_size, c * col_size), (row_size, col_size)
                    )
                    for c in cols
                ],
                axis=1,
            )
            for r in rows
        ],
        axis=0,
    )


def wide_device(green_top, factor_cols, fill_blocks, diag_inverse):
    row_index = lax.axis_index("row")
    col_index = lax.axis_index("col")
    row_count = lax.axis_size("row")
    col_count = lax.axis_size("col")
    local_rows, order = factor_cols.shape
    blocks = fill_blocks.shape[1]
    size = order // blocks
    group = blocks // col_count
    half = group // 2
    chunk = blocks // row_count
    exact = chunk % group == 0
    kept = chunk // 2 if exact else chunk

    def fill_of(k, start, count):
        return lax.dynamic_slice(fill_blocks, (k, start), (1, count))[0]

    def chosen(k, part):
        if exact:
            return filled(fill_of(k, part * chunk, chunk), kept)
        return list(range(kept))

    fill_line = jnp.repeat(fill_of(row_index, 0, blocks), size)
    masked = factor_cols * fill_line.astype(jnp.bfloat16)[None, :]
    picks = [[part * chunk + b for b in chosen(row_index, part)] for part in range(row_count)]
    own_factor = jnp.concatenate(
        [
            lax.dynamic_slice(masked, (0, b * size), (local_rows, size))
            for pick in picks
            for b in pick
        ],
        axis=1,
    )
    factor_parts = {t: partner(own_factor, "col", t) for t in range(1, col_count)}
    factor_parts[0] = own_factor

    green_parts = {}
    for s in range(row_count):
        k = row_index ^ s
        rows = filled(fill_of(k, col_index * group, group), half)
        green_parts[s] = cut(green_top, rows, size, chosen(k, row_index), size)
    for s in range(1, row_count):
        green_parts[s] = partner(green_parts[s], "row", s)

    factor = jnp.zeros((col_count * local_rows, own_factor.shape[1]), jnp.bfloat16)
    for t in range(col_count):
        factor = lax.dynamic_update_slice(
            factor, factor_parts[t], ((col_index ^ t) * local_rows, 0)
        )
    width = kept * size
    solved = 0.0
    for s in range(row_count):
        part = lax.dynamic_slice(
            factor, (0, (row_index ^ s) * width), (factor.shape[0], width)
        )
        solved = solved - lax.dot_general(
            part, green_parts[s], (((1,), (1,)), ((), ())), preferred_element_type=jnp.float32
        )
    fill_own = fill_of(row_index, col_index * group, group)
    rows = filled(fill_own, half)
    if exact:
        places = [col_index * half + p for p in range(half)]
    else:
        places = [col_index * group + r for r in rows]
    factor_rows = jnp.concatenate(
        [
            lax.dynamic_slice(factor, (0, b * size), (factor.shape[0], size))
            for b in places
        ],
        axis=1,
    )
    partial_value = lax.dot_general(
        solved,
        factor_rows.astype(jnp.float32),
        (((1,), (1,)), ((), ())),
        precision=lax.Precision.HIGHEST,
        preferred_element_type=jnp.float32,
    )
    rank = jnp.cumsum(fill_own) - 1
    green_cols = jnp.concatenate(
        [
            sum(
                jnp.where((fill_own[b] == 1) & (rank[b] == p), 1.0, 0.0)
                * solved[:, p * size : (p + 1) * size]
                for p in range(half)
            )
            for b in range(group)
        ],
        axis=1,
    )
    sums = [partial_value] + [partner(partial_value, "col", t) for t in range(1, col_count)]
    while len(sums) > 1:
        sums = [a + b for a, b in zip(sums[::2], sums[1::2])]
    return (green_cols, diag_inverse - sums[0])


def places(fill, k, start, count, wanted):
    found = [0] * wanted
    rank = 0
    for b in range(count):
        one = fill[k, start + b]
        for p in range(wanted):
            found[p] = jnp.where((one == 1) & (rank == p), b, found[p])
        rank = rank + one
    return found


def block(at, size):
    return pl.ds(pl.multiple_of(at * size, size), size)


def pack_kernel(
    row_count, col_count, fill_in, green_in, factor_in, own_factor, mask, *refs
):
    greens, (fill, green, factor, sems) = refs[:row_count], refs[row_count:]
    copies = [
        pltpu.make_async_copy(source, target, sems.at[n])
        for n, (source, target) in enumerate(
            [(fill_in, fill), (factor_in, factor), (green_in, green)]
        )
    ]
    for one in copies:
        one.start()
    row_index = lax.axis_index("row")
    col_index = lax.axis_index("col")
    blocks = fill.shape[1]
    size = factor.shape[1] // blocks
    group = blocks // col_count
    half = group // 2
    chunk = blocks // row_count
    kept = chunk // 2
    copies[0].wait()
    chosen = [
        (
            places(fill, row_index ^ s, col_index * group, group, half),
            places(fill, row_index ^ s, row_index * chunk, chunk, kept),
        )
        for s in range(row_count)
    ]
    own = [
        part * chunk + b
        for part in range(row_count)
        for b in places(fill, row_index, part * chunk, chunk, kept)
    ]
    for p, r in enumerate(chosen[0][0]):
        for b in range(group):
            mask[p : p + 1, b * size : (b + 1) * size] = jnp.full(
                (1, size), jnp.where(r == b, 1.0, 0.0), jnp.float32
            )
    copies[1].wait()
    for p, b in enumerate(own):
        own_factor[:, p * size : (p + 1) * size] = factor[:, block(b, size)]
    copies[2].wait()
    for s, (rows, cols) in enumerate(chosen):
        for p, r in enumerate(rows):
            for q, c in enumerate(cols):
                greens[s][p * size : (p + 1) * size, q * size : (q + 1) * size] = green[
                    block(r, size), block(c, size)
                ]


def pack(green_top, factor_cols, fill_blocks):
    row_count = lax.axis_size("row")
    col_count = lax.axis_size("col")
    local_rows, order = factor_cols.shape
    blocks = fill_blocks.shape[1]
    size = order // blocks
    group = blocks // col_count
    half = group // 2
    kept = blocks // row_count // 2
    shapes = [
        pltpu.VMEM((local_rows, row_count * kept * size), jnp.bfloat16),
        pltpu.VMEM((half, group * size), jnp.float32),
    ] + [pltpu.VMEM((half * size, kept * size), jnp.bfloat16)] * row_count
    return pl.pallas_call(
        lambda *refs: pack_kernel(row_count, col_count, *refs),
        out_shape=shapes,
        in_specs=[pl.BlockSpec(memory_space=pltpu.HBM)] * 3,
        out_specs=[pl.BlockSpec(memory_space=pltpu.VMEM)] * len(shapes),
        scratch_shapes=[
            pltpu.SMEM(fill_blocks.shape, fill_blocks.dtype),
            pltpu.VMEM(green_top.shape, green_top.dtype),
            pltpu.VMEM(factor_cols.shape, factor_cols.dtype),
            pltpu.SemaphoreType.DMA((3,)),
        ],
        name="pack",
    )(fill_blocks, green_top, factor_cols)


def code_of(value, coded):
    largest = jnp.max(jnp.abs(value), axis=0, keepdims=True)
    exponent = jnp.floor(jnp.log2(jnp.maximum(largest, 2.0**-100)))
    scaled = jnp.round(value * jnp.exp2(14.0 - exponent))
    count = value.shape[0]
    coded[:count, :] = jnp.clip(scaled, -32767.0, 32767.0).astype(jnp.int32).astype(jnp.int16)
    coded[count:, :] = jnp.broadcast_to(
        exponent.astype(jnp.int32), (EXPONENT_ROWS, value.shape[1])
    ).astype(jnp.int16)


def value_of(coded):
    count = coded.shape[0] - EXPONENT_ROWS
    exponent = coded[count:, :].astype(jnp.int32).astype(jnp.float32)[:1]
    return coded[:count, :].astype(jnp.int32).astype(jnp.float32) * jnp.exp2(exponent - 14.0)


def held_kernel(value, out):
    out[...] = value[...]


def held(value):
    return pl.pallas_call(
        held_kernel,
        out_shape=pltpu.VMEM(value.shape, value.dtype),
        in_specs=[pl.BlockSpec(memory_space=pltpu.VMEM)],
        out_specs=pl.BlockSpec(memory_space=pltpu.VMEM),
        compiler_params=pltpu.CompilerParams(vmem_limit_bytes=VMEM_LIMIT),
        cost_estimate=pl.CostEstimate(flops=10**9, bytes_accessed=1 << 20, transcendentals=0),
        name="held",
    )(value)


def gather_kernel(steps, own_factor, *refs):
    parts, factor = refs[: len(steps)], refs[-1]
    col_index = lax.axis_index("col")
    local_rows = own_factor.shape[0]
    for step, part in zip((0, *steps), (own_factor, *parts)):
        factor[block(col_index ^ step, local_rows), :] = part[...]


def solve_kernel(steps, factor, *refs):
    greens, (solved, coded) = refs[:-2], refs[-2:]
    row_index = lax.axis_index("row")
    col_index = lax.axis_index("col")
    rows, width = greens[0].shape
    total = jnp.zeros(solved.shape, jnp.float32)
    for step, green in zip(steps, greens):
        total = total + lax.dot_general(
            factor[:, block(row_index ^ step, width)],
            green[...],
            (((1,), (1,)), ((), ())),
            preferred_element_type=jnp.float32,
        )
    total = -total
    solved[...] = total
    pieces = []
    rest = total
    for _ in range(3):
        pieces.append(rest.astype(jnp.bfloat16))
        rest = rest - pieces[-1].astype(jnp.float32)
    own = factor[:, block(col_index, rows)]
    value = 0.0
    for piece in pieces[::-1]:
        value = value + lax.dot_general(
            piece, own, (((1,), (1,)), ((), ())), preferred_element_type=jnp.float32
        )
    code_of(value, coded)


def solve(own_factor, own_green, received, col_count):
    local_rows, columns = own_factor.shape
    count = col_count * local_rows
    params = pltpu.CompilerParams(vmem_limit_bytes=VMEM_LIMIT)
    vmem = pl.BlockSpec(memory_space=pltpu.VMEM)
    factors = [(step, part) for (axis, step), part in received.items() if axis == "col"]
    greens = [(step, part) for (axis, step), part in received.items() if axis == "row"]
    ahead = [part for step, part in greens if step != 1]
    factor = pl.pallas_call(
        lambda *refs: gather_kernel([step for step, _ in factors], *refs),
        out_shape=pltpu.VMEM((count, columns), jnp.bfloat16),
        in_specs=[vmem] * (1 + len(factors) + len(ahead)),
        out_specs=vmem,
        compiler_params=params,
        cost_estimate=pl.CostEstimate(flops=10**10, bytes_accessed=1 << 20, transcendentals=0),
        name="gather",
    )(own_factor, *[part for _, part in factors], *ahead)
    greens = [(0, own_green)] + sorted(greens, key=lambda one: one[0])
    return pl.pallas_call(
        lambda *refs: solve_kernel([step for step, _ in greens], *refs),
        out_shape=[
            pltpu.VMEM((count, own_green.shape[0]), jnp.float32),
            pltpu.VMEM((count + EXPONENT_ROWS, count), jnp.int16),
        ],
        in_specs=[vmem] * (1 + len(greens)),
        out_specs=[vmem] * 2,
        compiler_params=params,
        name="solve",
    )(factor, *[part for _, part in greens])


def finish_kernel(diag_inverse, own, back, across, ring, out):
    total = (value_of(own) + value_of(across)) + (value_of(ring) + value_of(back))
    out[...] = diag_inverse[...] - total


def finish(diag_inverse, codes):
    return pl.pallas_call(
        finish_kernel,
        out_shape=jax.ShapeDtypeStruct(diag_inverse.shape, diag_inverse.dtype),
        in_specs=[pl.BlockSpec(memory_space=pltpu.VMEM)] * (1 + len(codes)),
        out_specs=pl.BlockSpec(memory_space=pltpu.VMEM),
        compiler_params=pltpu.CompilerParams(vmem_limit_bytes=VMEM_LIMIT),
        name="finish",
    )(diag_inverse, *codes)


def per_device(green_top, factor_cols, fill_blocks, diag_inverse):
    row_count = lax.axis_size("row")
    col_count = lax.axis_size("col")
    blocks = fill_blocks.shape[1]
    chunk = blocks // row_count
    group = blocks // col_count
    fits = row_count == 4 and col_count == 4 and chunk % group == 0
    if not fits or green_top.size > 1 << 20:
        return wide_device(green_top, factor_cols, fill_blocks, diag_inverse)
    half = group // 2
    size = factor_cols.shape[1] // blocks

    own_factor, mask, *greens = pack(green_top, factor_cols, fill_blocks)
    transfers = {
        ("row", 2): partner(greens[2], "row", 2),
        ("row", 3): partner(greens[3], "row", 3),
        ("row", 1): partner(greens[1], "row", 1),
        ("col", 2): held(partner(own_factor, "col", 2)),
        ("col", 1): partner(own_factor, "col", 1),
        ("col", 3): partner(own_factor, "col", 3),
    }
    solved, code = solve(own_factor, greens[0], transfers, col_count)
    green_cols = None
    for p in range(half):
        term = mask[p : p + 1] * jnp.tile(solved[:, p * size : (p + 1) * size], (1, group))
        green_cols = term if green_cols is None else green_cols + term
    codes = [code] + [
        lax.ppermute(code, "col", list(enumerate(moves))) for moves in (BACK, ACROSS, RING)
    ]
    return (green_cols, finish(diag_inverse, codes))


def solution(mesh):
    placed = (
        P(("pole", "col"), "row"),
        P(("pole", "row", "col"), None),
        P(),
        P(("pole", "row"), None),
    )
    return jax.shard_map(
        per_device,
        mesh=mesh,
        in_specs=placed,
        out_specs=(P(("pole", "row"), "col"), P(("pole", "row"), None)),
        check_vma=False,
    )
```

```python
import jax
import jax.numpy as jnp
from jax import lax
from jax.experimental import pallas as pl
from jax.experimental.pallas import tpu as pltpu
from jax.sharding import PartitionSpec as P


EXPONENT_ROWS = 16
RING = (1, 3, 0, 2)
BACK = (2, 0, 3, 1)
ACROSS = (3, 2, 1, 0)
VMEM_LIMIT = 32 * 1024 * 1024


def partner(value, axis, step):
    size = lax.axis_size(axis)
    return lax.ppermute(value, axis, [(a, a ^ step) for a in range(size)])


def filled(line, count):
    rank = jnp.cumsum(line) - 1
    place = jnp.arange(line.shape[0])
    return [jnp.sum(jnp.where((line == 1) & (rank == p), place, 0)) for p in range(count)]


def cut(value, rows, row_size, cols, col_size):
    return jnp.concatenate(
        [
            jnp.concatenate(
                [
                    lax.dynamic_slice(
                        value, (r * row_size, c * col_size), (row_size, col_size)
                    )
                    for c in cols
                ],
                axis=1,
            )
            for r in rows
        ],
        axis=0,
    )


def wide_device(green_top, factor_cols, fill_blocks, diag_inverse):
    row_index = lax.axis_index("row")
    col_index = lax.axis_index("col")
    row_count = lax.axis_size("row")
    col_count = lax.axis_size("col")
    local_rows, order = factor_cols.shape
    blocks = fill_blocks.shape[1]
    size = order // blocks
    group = blocks // col_count
    half = group // 2
    chunk = blocks // row_count
    exact = chunk % group == 0
    kept = chunk // 2 if exact else chunk

    def fill_of(k, start, count):
        return lax.dynamic_slice(fill_blocks, (k, start), (1, count))[0]

    def chosen(k, part):
        if exact:
            return filled(fill_of(k, part * chunk, chunk), kept)
        return list(range(kept))

    fill_line = jnp.repeat(fill_of(row_index, 0, blocks), size)
    masked = factor_cols * fill_line.astype(jnp.bfloat16)[None, :]
    picks = [[part * chunk + b for b in chosen(row_index, part)] for part in range(row_count)]
    own_factor = jnp.concatenate(
        [
            lax.dynamic_slice(masked, (0, b * size), (local_rows, size))
            for pick in picks
            for b in pick
        ],
        axis=1,
    )
    factor_parts = {t: partner(own_factor, "col", t) for t in range(1, col_count)}
    factor_parts[0] = own_factor

    green_parts = {}
    for s in range(row_count):
        k = row_index ^ s
        rows = filled(fill_of(k, col_index * group, group), half)
        green_parts[s] = cut(green_top, rows, size, chosen(k, row_index), size)
    for s in range(1, row_count):
        green_parts[s] = partner(green_parts[s], "row", s)

    factor = jnp.zeros((col_count * local_rows, own_factor.shape[1]), jnp.bfloat16)
    for t in range(col_count):
        factor = lax.dynamic_update_slice(
            factor, factor_parts[t], ((col_index ^ t) * local_rows, 0)
        )
    width = kept * size
    solved = 0.0
    for s in range(row_count):
        part = lax.dynamic_slice(
            factor, (0, (row_index ^ s) * width), (factor.shape[0], width)
        )
        solved = solved - lax.dot_general(
            part, green_parts[s], (((1,), (1,)), ((), ())), preferred_element_type=jnp.float32
        )
    fill_own = fill_of(row_index, col_index * group, group)
    rows = filled(fill_own, half)
    if exact:
        places = [col_index * half + p for p in range(half)]
    else:
        places = [col_index * group + r for r in rows]
    factor_rows = jnp.concatenate(
        [
            lax.dynamic_slice(factor, (0, b * size), (factor.shape[0], size))
            for b in places
        ],
        axis=1,
    )
    partial_value = lax.dot_general(
        solved,
        factor_rows.astype(jnp.float32),
        (((1,), (1,)), ((), ())),
        precision=lax.Precision.HIGHEST,
        preferred_element_type=jnp.float32,
    )
    rank = jnp.cumsum(fill_own) - 1
    green_cols = jnp.concatenate(
        [
            sum(
                jnp.where((fill_own[b] == 1) & (rank[b] == p), 1.0, 0.0)
                * solved[:, p * size : (p + 1) * size]
                for p in range(half)
            )
            for b in range(group)
        ],
        axis=1,
    )
    sums = [partial_value] + [partner(partial_value, "col", t) for t in range(1, col_count)]
    while len(sums) > 1:
        sums = [a + b for a, b in zip(sums[::2], sums[1::2])]
    return (green_cols, diag_inverse - sums[0])


def places(fill, k, start, count, wanted):
    found = [0] * wanted
    rank = 0
    for b in range(count):
        one = fill[k, start + b]
        for p in range(wanted):
            found[p] = jnp.where((one == 1) & (rank == p), b, found[p])
        rank = rank + one
    return found


def block(at, size):
    return pl.ds(pl.multiple_of(at * size, size), size)


def pack_kernel(
    row_count, col_count, fill_in, green_in, factor_in, own_factor, mask, *refs
):
    greens, (fill, green, factor, sems) = refs[:row_count], refs[row_count:]
    copies = [
        pltpu.make_async_copy(source, target, sems.at[n])
        for n, (source, target) in enumerate(
            [(fill_in, fill), (factor_in, factor), (green_in, green)]
        )
    ]
    for one in copies:
        one.start()
    row_index = lax.axis_index("row")
    col_index = lax.axis_index("col")
    blocks = fill.shape[1]
    size = factor.shape[1] // blocks
    group = blocks // col_count
    half = group // 2
    chunk = blocks // row_count
    kept = chunk // 2
    copies[0].wait()
    chosen = [
        (
            places(fill, row_index ^ s, col_index * group, group, half),
            places(fill, row_index ^ s, row_index * chunk, chunk, kept),
        )
        for s in range(row_count)
    ]
    own = [
        part * chunk + b
        for part in range(row_count)
        for b in places(fill, row_index, part * chunk, chunk, kept)
    ]
    for p, r in enumerate(chosen[0][0]):
        for b in range(group):
            mask[p : p + 1, b * size : (b + 1) * size] = jnp.full(
                (1, size), jnp.where(r == b, 1.0, 0.0), jnp.float32
            )
    copies[1].wait()
    for p, b in enumerate(own):
        own_factor[:, p * size : (p + 1) * size] = factor[:, block(b, size)]
    copies[2].wait()
    for s, (rows, cols) in enumerate(chosen):
        for p, r in enumerate(rows):
            for q, c in enumerate(cols):
                greens[s][p * size : (p + 1) * size, q * size : (q + 1) * size] = green[
                    block(r, size), block(c, size)
                ]


def pack(green_top, factor_cols, fill_blocks):
    row_count = lax.axis_size("row")
    col_count = lax.axis_size("col")
    local_rows, order = factor_cols.shape
    blocks = fill_blocks.shape[1]
    size = order // blocks
    group = blocks // col_count
    half = group // 2
    kept = blocks // row_count // 2
    shapes = [
        pltpu.VMEM((local_rows, row_count * kept * size), jnp.bfloat16),
        pltpu.VMEM((half, group * size), jnp.float32),
    ] + [pltpu.VMEM((half * size, kept * size), jnp.bfloat16)] * row_count
    return pl.pallas_call(
        lambda *refs: pack_kernel(row_count, col_count, *refs),
        out_shape=shapes,
        in_specs=[pl.BlockSpec(memory_space=pltpu.HBM)] * 3,
        out_specs=[pl.BlockSpec(memory_space=pltpu.VMEM)] * len(shapes),
        scratch_shapes=[
            pltpu.SMEM(fill_blocks.shape, fill_blocks.dtype),
            pltpu.VMEM(green_top.shape, green_top.dtype),
            pltpu.VMEM(factor_cols.shape, factor_cols.dtype),
            pltpu.SemaphoreType.DMA((3,)),
        ],
        name="pack",
    )(fill_blocks, green_top, factor_cols)


def code_of(value, coded):
    largest = jnp.max(jnp.abs(value), axis=0, keepdims=True)
    exponent = jnp.floor(jnp.log2(jnp.maximum(largest, 2.0**-100)))
    scaled = jnp.round(value * jnp.exp2(14.0 - exponent))
    count = value.shape[0]
    coded[:count, :] = jnp.clip(scaled, -32767.0, 32767.0).astype(jnp.int32).astype(jnp.int16)
    coded[count:, :] = jnp.broadcast_to(
        exponent.astype(jnp.int32), (EXPONENT_ROWS, value.shape[1])
    ).astype(jnp.int16)


def value_of(coded):
    count = coded.shape[0] - EXPONENT_ROWS
    exponent = coded[count:, :].astype(jnp.int32).astype(jnp.float32)[:1]
    return coded[:count, :].astype(jnp.int32).astype(jnp.float32) * jnp.exp2(exponent - 14.0)


def solve_kernel(origins, own_factor, own_green, *refs):
    given, (solved, coded, factor) = refs[:-3], refs[-3:]
    row_index = lax.axis_index("row")
    col_index = lax.axis_index("col")
    local_rows = own_factor.shape[0]
    rows, width = own_green.shape
    greens = [(0, own_green)]
    factor[block(col_index, local_rows), :] = own_factor[...]
    for (axis, step), part in zip(origins, given):
        if axis == "col":
            factor[block(col_index ^ step, local_rows), :] = part[...]
        else:
            greens.append((step, part))
    total = jnp.zeros(solved.shape, jnp.float32)
    for step, green in sorted(greens, key=lambda one: one[0]):
        total = total + lax.dot_general(
            factor[:, block(row_index ^ step, width)],
            green[...],
            (((1,), (1,)), ((), ())),
            preferred_element_type=jnp.float32,
        )
    total = -total
    solved[...] = total
    pieces = []
    rest = total
    for _ in range(3):
        pieces.append(rest.astype(jnp.bfloat16))
        rest = rest - pieces[-1].astype(jnp.float32)
    own = factor[:, block(col_index, rows)]
    value = 0.0
    for piece in pieces[::-1]:
        value = value + lax.dot_general(
            piece, own, (((1,), (1,)), ((), ())), preferred_element_type=jnp.float32
        )
    code_of(value, coded)


def solve(own_factor, own_green, origins, given, col_count):
    local_rows, columns = own_factor.shape
    count = col_count * local_rows
    return pl.pallas_call(
        lambda *refs: solve_kernel(origins, *refs),
        out_shape=[
            pltpu.VMEM((count, own_green.shape[0]), jnp.float32),
            pltpu.VMEM((count + EXPONENT_ROWS, count), jnp.int16),
        ],
        in_specs=[pl.BlockSpec(memory_space=pltpu.VMEM)] * (2 + len(given)),
        out_specs=[pl.BlockSpec(memory_space=pltpu.VMEM)] * 2,
        scratch_shapes=[pltpu.VMEM((count, columns), jnp.bfloat16)],
        compiler_params=pltpu.CompilerParams(vmem_limit_bytes=VMEM_LIMIT),
        name="solve",
    )(own_factor, own_green, *given)


def finish_kernel(diag_inverse, own, back, across, ring, out):
    total = (value_of(own) + value_of(across)) + (value_of(ring) + value_of(back))
    out[...] = diag_inverse[...] - total


def finish(diag_inverse, codes):
    return pl.pallas_call(
        finish_kernel,
        out_shape=jax.ShapeDtypeStruct(diag_inverse.shape, diag_inverse.dtype),
        in_specs=[pl.BlockSpec(memory_space=pltpu.VMEM)] * (1 + len(codes)),
        out_specs=pl.BlockSpec(memory_space=pltpu.VMEM),
        compiler_params=pltpu.CompilerParams(vmem_limit_bytes=VMEM_LIMIT),
        name="finish",
    )(diag_inverse, *codes)


def per_device(green_top, factor_cols, fill_blocks, diag_inverse):
    row_count = lax.axis_size("row")
    col_count = lax.axis_size("col")
    blocks = fill_blocks.shape[1]
    chunk = blocks // row_count
    group = blocks // col_count
    fits = row_count == 4 and col_count == 4 and chunk % group == 0
    if not fits or green_top.size > 1 << 20:
        return wide_device(green_top, factor_cols, fill_blocks, diag_inverse)
    half = group // 2
    size = factor_cols.shape[1] // blocks

    own_factor, mask, *greens = pack(green_top, factor_cols, fill_blocks)
    second = partner(own_factor, "col", 2)
    received = {
        ("row", 2): partner(greens[2], "row", 2),
        ("row", 1): partner(greens[1], "row", 1),
        ("row", 3): partner(greens[3], "row", 3),
        ("col", 2): second,
        ("col", 1): partner(own_factor, "col", 1),
        ("col", 3): partner(second, "col", 1),
    }
    solved, code = solve(
        own_factor, greens[0], tuple(received), tuple(received.values()), col_count
    )
    green_cols = None
    for p in range(half):
        term = mask[p : p + 1] * jnp.tile(solved[:, p * size : (p + 1) * size], (1, group))
        green_cols = term if green_cols is None else green_cols + term
    codes = [code] + [
        lax.ppermute(code, "col", list(enumerate(moves))) for moves in (BACK, ACROSS, RING)
    ]
    return (green_cols, finish(diag_inverse, codes))


def solution(mesh):
    placed = (
        P(("pole", "col"), "row"),
        P(("pole", "row", "col"), None),
        P(),
        P(("pole", "row"), None),
    )
    return jax.shard_map(
        per_device,
        mesh=mesh,
        in_specs=placed,
        out_specs=(P(("pole", "row"), "col"), P(("pole", "row"), None)),
        check_vma=False,
    )
```

```python
import jax
import jax.numpy as jnp
from jax import lax
from jax.experimental import pallas as pl
from jax.experimental.pallas import tpu as pltpu
from jax.sharding import PartitionSpec as P


EXPONENT_ROWS = 16
RING = (1, 3, 0, 2)
BACK = (2, 0, 3, 1)
ACROSS = (3, 2, 1, 0)
VMEM_LIMIT = 32 * 1024 * 1024


def partner(value, axis, step):
    size = lax.axis_size(axis)
    return lax.ppermute(value, axis, [(a, a ^ step) for a in range(size)])


def filled(line, count):
    rank = jnp.cumsum(line) - 1
    place = jnp.arange(line.shape[0])
    return [jnp.sum(jnp.where((line == 1) & (rank == p), place, 0)) for p in range(count)]


def cut(value, rows, row_size, cols, col_size):
    return jnp.concatenate(
        [
            jnp.concatenate(
                [
                    lax.dynamic_slice(
                        value, (r * row_size, c * col_size), (row_size, col_size)
                    )
                    for c in cols
                ],
                axis=1,
            )
            for r in rows
        ],
        axis=0,
    )


def wide_device(green_top, factor_cols, fill_blocks, diag_inverse):
    row_index = lax.axis_index("row")
    col_index = lax.axis_index("col")
    row_count = lax.axis_size("row")
    col_count = lax.axis_size("col")
    local_rows, order = factor_cols.shape
    blocks = fill_blocks.shape[1]
    size = order // blocks
    group = blocks // col_count
    half = group // 2
    chunk = blocks // row_count
    exact = chunk % group == 0
    kept = chunk // 2 if exact else chunk

    def fill_of(k, start, count):
        return lax.dynamic_slice(fill_blocks, (k, start), (1, count))[0]

    def chosen(k, part):
        if exact:
            return filled(fill_of(k, part * chunk, chunk), kept)
        return list(range(kept))

    fill_line = jnp.repeat(fill_of(row_index, 0, blocks), size)
    masked = factor_cols * fill_line.astype(jnp.bfloat16)[None, :]
    picks = [[part * chunk + b for b in chosen(row_index, part)] for part in range(row_count)]
    own_factor = jnp.concatenate(
        [
            lax.dynamic_slice(masked, (0, b * size), (local_rows, size))
            for pick in picks
            for b in pick
        ],
        axis=1,
    )
    factor_parts = {t: partner(own_factor, "col", t) for t in range(1, col_count)}
    factor_parts[0] = own_factor

    green_parts = {}
    for s in range(row_count):
        k = row_index ^ s
        rows = filled(fill_of(k, col_index * group, group), half)
        green_parts[s] = cut(green_top, rows, size, chosen(k, row_index), size)
    for s in range(1, row_count):
        green_parts[s] = partner(green_parts[s], "row", s)

    factor = jnp.zeros((col_count * local_rows, own_factor.shape[1]), jnp.bfloat16)
    for t in range(col_count):
        factor = lax.dynamic_update_slice(
            factor, factor_parts[t], ((col_index ^ t) * local_rows, 0)
        )
    width = kept * size
    solved = 0.0
    for s in range(row_count):
        part = lax.dynamic_slice(
            factor, (0, (row_index ^ s) * width), (factor.shape[0], width)
        )
        solved = solved - lax.dot_general(
            part, green_parts[s], (((1,), (1,)), ((), ())), preferred_element_type=jnp.float32
        )
    fill_own = fill_of(row_index, col_index * group, group)
    rows = filled(fill_own, half)
    if exact:
        places = [col_index * half + p for p in range(half)]
    else:
        places = [col_index * group + r for r in rows]
    factor_rows = jnp.concatenate(
        [
            lax.dynamic_slice(factor, (0, b * size), (factor.shape[0], size))
            for b in places
        ],
        axis=1,
    )
    partial_value = lax.dot_general(
        solved,
        factor_rows.astype(jnp.float32),
        (((1,), (1,)), ((), ())),
        precision=lax.Precision.HIGHEST,
        preferred_element_type=jnp.float32,
    )
    rank = jnp.cumsum(fill_own) - 1
    green_cols = jnp.concatenate(
        [
            sum(
                jnp.where((fill_own[b] == 1) & (rank[b] == p), 1.0, 0.0)
                * solved[:, p * size : (p + 1) * size]
                for p in range(half)
            )
            for b in range(group)
        ],
        axis=1,
    )
    sums = [partial_value] + [partner(partial_value, "col", t) for t in range(1, col_count)]
    while len(sums) > 1:
        sums = [a + b for a, b in zip(sums[::2], sums[1::2])]
    return (green_cols, diag_inverse - sums[0])


def places(fill, k, start, count, wanted):
    found = [0] * wanted
    rank = 0
    for b in range(count):
        one = fill[k, start + b]
        for p in range(wanted):
            found[p] = jnp.where((one == 1) & (rank == p), b, found[p])
        rank = rank + one
    return found


def block(at, size):
    return pl.ds(pl.multiple_of(at * size, size), size)


def pack_kernel(
    row_count, col_count, fill_in, green_in, factor_in, own_factor, mask, *refs
):
    greens, (fill, green, factor, sems) = refs[:row_count], refs[row_count:]
    copies = [
        pltpu.make_async_copy(source, target, sems.at[n])
        for n, (source, target) in enumerate(
            [(fill_in, fill), (factor_in, factor), (green_in, green)]
        )
    ]
    for one in copies:
        one.start()
    row_index = lax.axis_index("row")
    col_index = lax.axis_index("col")
    blocks = fill.shape[1]
    size = factor.shape[1] // blocks
    group = blocks // col_count
    half = group // 2
    chunk = blocks // row_count
    kept = chunk // 2
    copies[0].wait()
    chosen = [
        (
            places(fill, row_index ^ s, col_index * group, group, half),
            places(fill, row_index ^ s, row_index * chunk, chunk, kept),
        )
        for s in range(row_count)
    ]
    own = [
        part * chunk + b
        for part in range(row_count)
        for b in places(fill, row_index, part * chunk, chunk, kept)
    ]
    for p, r in enumerate(chosen[0][0]):
        for b in range(group):
            mask[p : p + 1, b * size : (b + 1) * size] = jnp.full(
                (1, size), jnp.where(r == b, 1.0, 0.0), jnp.float32
            )
    copies[1].wait()
    for p, b in enumerate(own):
        own_factor[:, p * size : (p + 1) * size] = factor[:, block(b, size)]
    copies[2].wait()
    for s, (rows, cols) in enumerate(chosen):
        for p, r in enumerate(rows):
            for q, c in enumerate(cols):
                greens[s][p * size : (p + 1) * size, q * size : (q + 1) * size] = green[
                    block(r, size), block(c, size)
                ]


def pack(green_top, factor_cols, fill_blocks):
    row_count = lax.axis_size("row")
    col_count = lax.axis_size("col")
    local_rows, order = factor_cols.shape
    blocks = fill_blocks.shape[1]
    size = order // blocks
    group = blocks // col_count
    half = group // 2
    kept = blocks // row_count // 2
    shapes = [
        pltpu.VMEM((local_rows, row_count * kept * size), jnp.bfloat16),
        pltpu.VMEM((half, group * size), jnp.float32),
    ] + [pltpu.VMEM((half * size, kept * size), jnp.bfloat16)] * row_count
    return pl.pallas_call(
        lambda *refs: pack_kernel(row_count, col_count, *refs),
        out_shape=shapes,
        in_specs=[pl.BlockSpec(memory_space=pltpu.HBM)] * 3,
        out_specs=[pl.BlockSpec(memory_space=pltpu.VMEM)] * len(shapes),
        scratch_shapes=[
            pltpu.SMEM(fill_blocks.shape, fill_blocks.dtype),
            pltpu.VMEM(green_top.shape, green_top.dtype),
            pltpu.VMEM(factor_cols.shape, factor_cols.dtype),
            pltpu.SemaphoreType.DMA((3,)),
        ],
        name="pack",
    )(fill_blocks, green_top, factor_cols)


def code_of(value, coded):
    largest = jnp.max(jnp.abs(value), axis=0, keepdims=True)
    exponent = jnp.floor(jnp.log2(jnp.maximum(largest, 2.0**-100)))
    scaled = jnp.round(value * jnp.exp2(14.0 - exponent))
    count = value.shape[0]
    coded[:count, :] = jnp.clip(scaled, -32767.0, 32767.0).astype(jnp.int32).astype(jnp.int16)
    coded[count:, :] = jnp.broadcast_to(
        exponent.astype(jnp.int32), (EXPONENT_ROWS, value.shape[1])
    ).astype(jnp.int16)


def value_of(coded):
    count = coded.shape[0] - EXPONENT_ROWS
    exponent = coded[count:, :].astype(jnp.int32).astype(jnp.float32)[:1]
    return coded[:count, :].astype(jnp.int32).astype(jnp.float32) * jnp.exp2(exponent - 14.0)


def solve_kernel(origins, own_factor, own_green, *refs):
    given, (solved, coded, factor) = refs[:-3], refs[-3:]
    row_index = lax.axis_index("row")
    col_index = lax.axis_index("col")
    local_rows = own_factor.shape[0]
    rows, width = own_green.shape
    greens = [(0, own_green)]
    factor[block(col_index, local_rows), :] = own_factor[...]
    for (axis, step), part in zip(origins, given):
        if axis == "col":
            factor[block(col_index ^ step, local_rows), :] = part[...]
        else:
            greens.append((step, part))
    greens = sorted(greens, key=lambda one: one[0])
    total = lax.dot_general(
        jnp.concatenate([factor[:, block(row_index ^ step, width)] for step, _ in greens], axis=1),
        jnp.concatenate([green[...] for _, green in greens], axis=1),
        (((1,), (1,)), ((), ())),
        preferred_element_type=jnp.float32,
    )
    total = -total
    solved[...] = total
    pieces = []
    rest = total
    for _ in range(3):
        pieces.append(rest.astype(jnp.bfloat16))
        rest = rest - pieces[-1].astype(jnp.float32)
    own = factor[:, block(col_index, rows)]
    value = lax.dot_general(
        jnp.concatenate(pieces[::-1], axis=1),
        jnp.concatenate([own] * len(pieces), axis=1),
        (((1,), (1,)), ((), ())),
        preferred_element_type=jnp.float32,
    )
    code_of(value, coded)


def solve(own_factor, own_green, origins, given, col_count):
    local_rows, columns = own_factor.shape
    count = col_count * local_rows
    return pl.pallas_call(
        lambda *refs: solve_kernel(origins, *refs),
        out_shape=[
            pltpu.VMEM((count, own_green.shape[0]), jnp.float32),
            pltpu.VMEM((count + EXPONENT_ROWS, count), jnp.int16),
        ],
        in_specs=[pl.BlockSpec(memory_space=pltpu.VMEM)] * (2 + len(given)),
        out_specs=[pl.BlockSpec(memory_space=pltpu.VMEM)] * 2,
        scratch_shapes=[pltpu.VMEM((count, columns), jnp.bfloat16)],
        compiler_params=pltpu.CompilerParams(vmem_limit_bytes=VMEM_LIMIT),
        name="solve",
    )(own_factor, own_green, *given)


def finish_kernel(diag_inverse, own, back, across, ring, out):
    total = (value_of(own) + value_of(across)) + (value_of(ring) + value_of(back))
    out[...] = diag_inverse[...] - total


def finish(diag_inverse, codes):
    return pl.pallas_call(
        finish_kernel,
        out_shape=jax.ShapeDtypeStruct(diag_inverse.shape, diag_inverse.dtype),
        in_specs=[pl.BlockSpec(memory_space=pltpu.VMEM)] * (1 + len(codes)),
        out_specs=pl.BlockSpec(memory_space=pltpu.VMEM),
        compiler_params=pltpu.CompilerParams(vmem_limit_bytes=VMEM_LIMIT),
        name="finish",
    )(diag_inverse, *codes)


def per_device(green_top, factor_cols, fill_blocks, diag_inverse):
    row_count = lax.axis_size("row")
    col_count = lax.axis_size("col")
    blocks = fill_blocks.shape[1]
    chunk = blocks // row_count
    group = blocks // col_count
    fits = row_count == 4 and col_count == 4 and chunk % group == 0
    if not fits or green_top.size > 1 << 20:
        return wide_device(green_top, factor_cols, fill_blocks, diag_inverse)
    half = group // 2
    size = factor_cols.shape[1] // blocks

    own_factor, mask, *greens = pack(green_top, factor_cols, fill_blocks)
    second = partner(own_factor, "col", 2)
    received = {
        ("row", 2): partner(greens[2], "row", 2),
        ("row", 3): partner(greens[3], "row", 3),
        ("row", 1): partner(greens[1], "row", 1),
        ("col", 2): second,
        ("col", 1): partner(own_factor, "col", 1),
        ("col", 3): partner(second, "col", 1),
    }
    solved, code = solve(
        own_factor, greens[0], tuple(received), tuple(received.values()), col_count
    )
    green_cols = None
    for p in range(half):
        term = mask[p : p + 1] * jnp.tile(solved[:, p * size : (p + 1) * size], (1, group))
        green_cols = term if green_cols is None else green_cols + term
    codes = [code] + [
        lax.ppermute(code, "col", list(enumerate(moves))) for moves in (BACK, ACROSS, RING)
    ]
    return (green_cols, finish(diag_inverse, codes))


def solution(mesh):
    placed = (
        P(("pole", "col"), "row"),
        P(("pole", "row", "col"), None),
        P(),
        P(("pole", "row"), None),
    )
    return jax.shard_map(
        per_device,
        mesh=mesh,
        in_specs=placed,
        out_specs=(P(("pole", "row"), "col"), P(("pole", "row"), None)),
        check_vma=False,
    )
```

```python
import jax
import jax.numpy as jnp
from jax import lax
from jax.experimental import pallas as pl
from jax.experimental.pallas import tpu as pltpu
from jax.sharding import PartitionSpec as P


EXPONENT_ROWS = 16
ROW_MOVES = ((0, 1, 2, 3), (3, 2, 0, 1), (1, 0, 3, 2), (2, 3, 1, 0))


def looked_up(table, index):
    return sum(jnp.where(index == a, b, 0) for a, b in enumerate(table))


def sources(table):
    return [table.index(a) for a in range(len(table))]
OPERANDS = (0, 4, 5, 6, 7, 1, 2, 3)


def partner(value, axis, step):
    size = lax.axis_size(axis)
    return lax.ppermute(value, axis, [(a, a ^ step) for a in range(size)])


def filled(line, count):
    rank = jnp.cumsum(line) - 1
    place = jnp.arange(line.shape[0])
    return [jnp.sum(jnp.where((line == 1) & (rank == p), place, 0)) for p in range(count)]


def cut(value, rows, row_size, cols, col_size):
    return jnp.concatenate(
        [
            jnp.concatenate(
                [
                    lax.dynamic_slice(
                        value, (r * row_size, c * col_size), (row_size, col_size)
                    )
                    for c in cols
                ],
                axis=1,
            )
            for r in rows
        ],
        axis=0,
    )


def wide_device(green_top, factor_cols, fill_blocks, diag_inverse):
    row_index = lax.axis_index("row")
    col_index = lax.axis_index("col")
    row_count = lax.axis_size("row")
    col_count = lax.axis_size("col")
    local_rows, order = factor_cols.shape
    blocks = fill_blocks.shape[1]
    size = order // blocks
    group = blocks // col_count
    half = group // 2
    chunk = blocks // row_count
    exact = chunk % group == 0
    kept = chunk // 2 if exact else chunk

    def fill_of(k, start, count):
        return lax.dynamic_slice(fill_blocks, (k, start), (1, count))[0]

    def chosen(k, part):
        if exact:
            return filled(fill_of(k, part * chunk, chunk), kept)
        return list(range(kept))

    fill_line = jnp.repeat(fill_of(row_index, 0, blocks), size)
    masked = factor_cols * fill_line.astype(jnp.bfloat16)[None, :]
    picks = [[part * chunk + b for b in chosen(row_index, part)] for part in range(row_count)]
    own_factor = jnp.concatenate(
        [
            lax.dynamic_slice(masked, (0, b * size), (local_rows, size))
            for pick in picks
            for b in pick
        ],
        axis=1,
    )
    factor_parts = {t: partner(own_factor, "col", t) for t in range(1, col_count)}
    factor_parts[0] = own_factor

    green_parts = {}
    for s in range(row_count):
        k = row_index ^ s
        rows = filled(fill_of(k, col_index * group, group), half)
        green_parts[s] = cut(green_top, rows, size, chosen(k, row_index), size)
    for s in range(1, row_count):
        green_parts[s] = partner(green_parts[s], "row", s)

    factor = jnp.zeros((col_count * local_rows, own_factor.shape[1]), jnp.bfloat16)
    for t in range(col_count):
        factor = lax.dynamic_update_slice(
            factor, factor_parts[t], ((col_index ^ t) * local_rows, 0)
        )
    width = kept * size
    solved = 0.0
    for s in range(row_count):
        part = lax.dynamic_slice(
            factor, (0, (row_index ^ s) * width), (factor.shape[0], width)
        )
        solved = solved - lax.dot_general(
            part, green_parts[s], (((1,), (1,)), ((), ())), preferred_element_type=jnp.float32
        )
    fill_own = fill_of(row_index, col_index * group, group)
    rows = filled(fill_own, half)
    if exact:
        places = [col_index * half + p for p in range(half)]
    else:
        places = [col_index * group + r for r in rows]
    factor_rows = jnp.concatenate(
        [
            lax.dynamic_slice(factor, (0, b * size), (factor.shape[0], size))
            for b in places
        ],
        axis=1,
    )
    partial_value = lax.dot_general(
        solved,
        factor_rows.astype(jnp.float32),
        (((1,), (1,)), ((), ())),
        precision=lax.Precision.HIGHEST,
        preferred_element_type=jnp.float32,
    )
    rank = jnp.cumsum(fill_own) - 1
    green_cols = jnp.concatenate(
        [
            sum(
                jnp.where((fill_own[b] == 1) & (rank[b] == p), 1.0, 0.0)
                * solved[:, p * size : (p + 1) * size]
                for p in range(half)
            )
            for b in range(group)
        ],
        axis=1,
    )
    sums = [partial_value] + [partner(partial_value, "col", t) for t in range(1, col_count)]
    while len(sums) > 1:
        sums = [a + b for a, b in zip(sums[::2], sums[1::2])]
    return (green_cols, diag_inverse - sums[0])


def places(fill, k, start, count, wanted):
    found = [0] * wanted
    rank = 0
    for b in range(count):
        one = fill[k, start + b]
        for p in range(wanted):
            found[p] = jnp.where((one == 1) & (rank == p), b, found[p])
        rank = rank + one
    return found


def block(at, size):
    return pl.ds(pl.multiple_of(at * size, size), size)


def pack_kernel(
    row_count, col_count, fill_in, green_in, factor_in, own_factor, mask, *refs
):
    greens, (fill, green, factor, sems) = refs[:row_count], refs[row_count:]
    copies = [
        pltpu.make_async_copy(source, target, sems.at[n])
        for n, (source, target) in enumerate(
            [(fill_in, fill), (factor_in, factor), (green_in, green)]
        )
    ]
    for one in copies:
        one.start()
    row_index = lax.axis_index("row")
    col_index = lax.axis_index("col")
    blocks = fill.shape[1]
    size = factor.shape[1] // blocks
    group = blocks // col_count
    half = group // 2
    chunk = blocks // row_count
    kept = chunk // 2
    copies[0].wait()
    chosen = [
        (
            places(fill, looked_up(ROW_MOVES[s], row_index), col_index * group, group, half),
            places(fill, looked_up(ROW_MOVES[s], row_index), row_index * chunk, chunk, kept),
        )
        for s in range(row_count)
    ]
    own = [
        part * chunk + b
        for part in range(row_count)
        for b in places(fill, row_index, part * chunk, chunk, kept)
    ]
    for p, r in enumerate(chosen[0][0]):
        for b in range(group):
            mask[p : p + 1, b * size : (b + 1) * size] = jnp.full(
                (1, size), jnp.where(r == b, 1.0, 0.0), jnp.float32
            )
    copies[1].wait()
    for p, b in enumerate(own):
        own_factor[:, p * size : (p + 1) * size] = factor[:, block(b, size)]
    copies[2].wait()
    for s, (rows, cols) in enumerate(chosen):
        for p, r in enumerate(rows):
            for q, c in enumerate(cols):
                greens[s][p * size : (p + 1) * size, q * size : (q + 1) * size] = green[
                    block(r, size), block(c, size)
                ]


def pack(green_top, factor_cols, fill_blocks):
    row_count = lax.axis_size("row")
    col_count = lax.axis_size("col")
    local_rows, order = factor_cols.shape
    blocks = fill_blocks.shape[1]
    size = order // blocks
    group = blocks // col_count
    half = group // 2
    kept = blocks // row_count // 2
    shapes = [
        pltpu.VMEM((local_rows, row_count * kept * size), jnp.bfloat16),
        pltpu.VMEM((half, group * size), jnp.float32),
    ] + [pltpu.VMEM((half * size, kept * size), jnp.bfloat16)] * row_count
    return pl.pallas_call(
        lambda *refs: pack_kernel(row_count, col_count, *refs),
        out_shape=shapes,
        in_specs=[pl.BlockSpec(memory_space=pltpu.HBM)] * 3,
        out_specs=[pl.BlockSpec(memory_space=pltpu.VMEM)] * len(shapes),
        scratch_shapes=[
            pltpu.SMEM(fill_blocks.shape, fill_blocks.dtype),
            pltpu.VMEM(green_top.shape, green_top.dtype),
            pltpu.VMEM(factor_cols.shape, factor_cols.dtype),
            pltpu.SemaphoreType.DMA((3,)),
        ],
        name="pack",
    )(fill_blocks, green_top, factor_cols)


def split(given, row_count, col_count):
    order = OPERANDS if (row_count, col_count) == (4, 4) else range(row_count + col_count)
    placed = dict(zip(order, given))
    return [placed[n] for n in range(col_count)], [
        placed[col_count + n] for n in range(row_count)
    ]


def solve_kernel(row_count, col_count, *refs):
    given, (solved, coded, factor) = refs[: row_count + col_count], refs[row_count + col_count :]
    factors, greens = split(given, row_count, col_count)
    row_index = lax.axis_index("row")
    col_index = lax.axis_index("col")
    local_rows = factors[0].shape[0]
    rows, width = greens[0].shape
    origins = [(0, 1, 2, 3)] + [(2, 3, 0, 1), (1, 0, 3, 2), (3, 2, 1, 0)]
    for origin, part in zip(origins, factors):
        place = sum(jnp.where(col_index == a, o, 0) for a, o in enumerate(origin))
        factor[block(place, local_rows), :] = part[...]
    total = jnp.zeros(solved.shape, jnp.float32)
    for s in range(row_count):
        total = total + lax.dot_general(
            factor[:, block(looked_up(sources(ROW_MOVES[s]), row_index), width)],
            greens[s][...],
            (((1,), (1,)), ((), ())),
            preferred_element_type=jnp.float32,
        )
    total = -total
    solved[...] = total
    pieces = []
    rest = total
    for _ in range(3):
        pieces.append(rest.astype(jnp.bfloat16))
        rest = rest - pieces[-1].astype(jnp.float32)
    own = factor[:, block(col_index, rows)]
    value = 0.0
    for piece in pieces[::-1]:
        value = value + lax.dot_general(
            piece, own, (((1,), (1,)), ((), ())), preferred_element_type=jnp.float32
        )
    largest = jnp.max(jnp.abs(value), axis=0, keepdims=True)
    exponent = jnp.floor(jnp.log2(jnp.maximum(largest, 2.0**-100)))
    scaled = jnp.round(value * jnp.exp2(14.0 - exponent))
    count = value.shape[0]
    coded[:count, :] = jnp.clip(scaled, -32767.0, 32767.0).astype(jnp.int32).astype(jnp.int16)
    coded[count:, :] = jnp.broadcast_to(
        exponent.astype(jnp.int32), (EXPONENT_ROWS, value.shape[1])
    ).astype(jnp.int16)


def solve(factors, greens):
    col_count, row_count = len(factors), len(greens)
    local_rows, columns = factors[0].shape
    count = col_count * local_rows
    return pl.pallas_call(
        lambda *refs: solve_kernel(row_count, col_count, *refs),
        out_shape=[
            pltpu.VMEM((count, greens[0].shape[0]), jnp.float32),
            pltpu.VMEM((count + EXPONENT_ROWS, count), jnp.int16),
        ],
        in_specs=[pl.BlockSpec(memory_space=pltpu.VMEM)] * (row_count + col_count),
        out_specs=[pl.BlockSpec(memory_space=pltpu.VMEM)] * 2,
        scratch_shapes=[pltpu.VMEM((count, columns), jnp.bfloat16)],
        compiler_params=pltpu.CompilerParams(vmem_limit_bytes=32 * 1024 * 1024),
        name="solve",
    )(*[(list(factors) + list(greens))[n] for n in (OPERANDS if (row_count, col_count) == (4, 4) else range(row_count + col_count))])


def finish_kernel(diag_inverse, *refs):
    codes, out = refs[:-1], refs[-1]
    count = diag_inverse.shape[0]
    sums = []
    for code in codes:
        exponent = code[count:, :].astype(jnp.int32).astype(jnp.float32)[:1]
        sums.append(code[:count, :].astype(jnp.int32).astype(jnp.float32) * jnp.exp2(exponent - 14.0))
    total = (sums[0] + sums[2]) + (sums[3] + sums[1])
    out[...] = diag_inverse[...] - total


def finish(diag_inverse, codes):
    return pl.pallas_call(
        finish_kernel,
        out_shape=jax.ShapeDtypeStruct(diag_inverse.shape, diag_inverse.dtype),
        in_specs=[pl.BlockSpec(memory_space=pltpu.VMEM)] * (1 + len(codes)),
        out_specs=pl.BlockSpec(memory_space=pltpu.VMEM),
        compiler_params=pltpu.CompilerParams(vmem_limit_bytes=32 * 1024 * 1024),
        name="finish",
    )(diag_inverse, *codes)


def per_device(green_top, factor_cols, fill_blocks, diag_inverse):
    row_count = lax.axis_size("row")
    col_count = lax.axis_size("col")
    blocks = fill_blocks.shape[1]
    chunk = blocks // row_count
    group = blocks // col_count
    if chunk % group or green_top.size > 1 << 20:
        return wide_device(green_top, factor_cols, fill_blocks, diag_inverse)
    half = group // 2
    size = factor_cols.shape[1] // blocks

    own_factor, mask, *greens = pack(green_top, factor_cols, fill_blocks)
    moves = {
        "b+": (1, 3, 0, 2),
        "b-": (2, 0, 3, 1),
        "z1": (1, 0, 3, 2),
        "z2": (2, 3, 0, 1),
        "z3": (3, 2, 1, 0),
    }

    def moved(value, name):
        return lax.ppermute(value, "col", list(enumerate(moves[name])))

    def crossed(value, m):
        return lax.ppermute(value, "row", list(enumerate(ROW_MOVES[m])))

    parts = {n: crossed(greens[m], m) for m, n in ((1, "c"), (2, "x"), (3, "xc"))}
    parts["z1"] = moved(own_factor, "z1")
    parts["z2"] = moved(own_factor, "z2")
    passed, *rest = lax.optimization_barrier((parts["z2"], *[parts[n] for n in []]))
    parts.update(zip([], rest))
    parts["fw"] = moved(passed, "z1")
    greens = [greens[0], parts["c"], parts["x"], parts["xc"]]
    factors = [own_factor] + [parts[n] for n in ['z2', 'z1', 'fw']]
    solved, code = solve(factors, greens)
    green_cols = None
    for p in range(half):
        term = mask[p : p + 1] * jnp.tile(solved[:, p * size : (p + 1) * size], (1, group))
        green_cols = term if green_cols is None else green_cols + term
    codes = [code] + [moved(code, name) for name in ['b-', 'z3', 'b+']]
    return (green_cols, finish(diag_inverse, codes))


def solution(mesh):
    placed = (
        P(("pole", "col"), "row"),
        P(("pole", "row", "col"), None),
        P(),
        P(("pole", "row"), None),
    )
    return jax.shard_map(
        per_device,
        mesh=mesh,
        in_specs=placed,
        out_specs=(P(("pole", "row"), "col"), P(("pole", "row"), None)),
        check_vma=False,
    )
```

```python
import jax
import jax.numpy as jnp
from jax import lax
from jax.experimental import pallas as pl
from jax.experimental.pallas import tpu as pltpu
from jax.sharding import PartitionSpec as P


EXPONENT_ROWS = 16
ROW_MOVES = ((0, 1, 2, 3), (3, 2, 0, 1), (1, 0, 3, 2), (2, 3, 1, 0))


def looked_up(table, index):
    return sum(jnp.where(index == a, b, 0) for a, b in enumerate(table))


def sources(table):
    return [table.index(a) for a in range(len(table))]
OPERANDS = (0, 4, 5, 6, 7, 1, 2, 3)


def partner(value, axis, step):
    size = lax.axis_size(axis)
    return lax.ppermute(value, axis, [(a, a ^ step) for a in range(size)])


def filled(line, count):
    rank = jnp.cumsum(line) - 1
    place = jnp.arange(line.shape[0])
    return [jnp.sum(jnp.where((line == 1) & (rank == p), place, 0)) for p in range(count)]


def cut(value, rows, row_size, cols, col_size):
    return jnp.concatenate(
        [
            jnp.concatenate(
                [
                    lax.dynamic_slice(
                        value, (r * row_size, c * col_size), (row_size, col_size)
                    )
                    for c in cols
                ],
                axis=1,
            )
            for r in rows
        ],
        axis=0,
    )


def wide_device(green_top, factor_cols, fill_blocks, diag_inverse):
    row_index = lax.axis_index("row")
    col_index = lax.axis_index("col")
    row_count = lax.axis_size("row")
    col_count = lax.axis_size("col")
    local_rows, order = factor_cols.shape
    blocks = fill_blocks.shape[1]
    size = order // blocks
    group = blocks // col_count
    half = group // 2
    chunk = blocks // row_count
    exact = chunk % group == 0
    kept = chunk // 2 if exact else chunk

    def fill_of(k, start, count):
        return lax.dynamic_slice(fill_blocks, (k, start), (1, count))[0]

    def chosen(k, part):
        if exact:
            return filled(fill_of(k, part * chunk, chunk), kept)
        return list(range(kept))

    fill_line = jnp.repeat(fill_of(row_index, 0, blocks), size)
    masked = factor_cols * fill_line.astype(jnp.bfloat16)[None, :]
    picks = [[part * chunk + b for b in chosen(row_index, part)] for part in range(row_count)]
    own_factor = jnp.concatenate(
        [
            lax.dynamic_slice(masked, (0, b * size), (local_rows, size))
            for pick in picks
            for b in pick
        ],
        axis=1,
    )
    factor_parts = {t: partner(own_factor, "col", t) for t in range(1, col_count)}
    factor_parts[0] = own_factor

    green_parts = {}
    for s in range(row_count):
        k = row_index ^ s
        rows = filled(fill_of(k, col_index * group, group), half)
        green_parts[s] = cut(green_top, rows, size, chosen(k, row_index), size)
    for s in range(1, row_count):
        green_parts[s] = partner(green_parts[s], "row", s)

    factor = jnp.zeros((col_count * local_rows, own_factor.shape[1]), jnp.bfloat16)
    for t in range(col_count):
        factor = lax.dynamic_update_slice(
            factor, factor_parts[t], ((col_index ^ t) * local_rows, 0)
        )
    width = kept * size
    solved = 0.0
    for s in range(row_count):
        part = lax.dynamic_slice(
            factor, (0, (row_index ^ s) * width), (factor.shape[0], width)
        )
        solved = solved - lax.dot_general(
            part, green_parts[s], (((1,), (1,)), ((), ())), preferred_element_type=jnp.float32
        )
    fill_own = fill_of(row_index, col_index * group, group)
    rows = filled(fill_own, half)
    if exact:
        places = [col_index * half + p for p in range(half)]
    else:
        places = [col_index * group + r for r in rows]
    factor_rows = jnp.concatenate(
        [
            lax.dynamic_slice(factor, (0, b * size), (factor.shape[0], size))
            for b in places
        ],
        axis=1,
    )
    partial_value = lax.dot_general(
        solved,
        factor_rows.astype(jnp.float32),
        (((1,), (1,)), ((), ())),
        precision=lax.Precision.HIGHEST,
        preferred_element_type=jnp.float32,
    )
    rank = jnp.cumsum(fill_own) - 1
    green_cols = jnp.concatenate(
        [
            sum(
                jnp.where((fill_own[b] == 1) & (rank[b] == p), 1.0, 0.0)
                * solved[:, p * size : (p + 1) * size]
                for p in range(half)
            )
            for b in range(group)
        ],
        axis=1,
    )
    sums = [partial_value] + [partner(partial_value, "col", t) for t in range(1, col_count)]
    while len(sums) > 1:
        sums = [a + b for a, b in zip(sums[::2], sums[1::2])]
    return (green_cols, diag_inverse - sums[0])


def places(fill, k, start, count, wanted):
    found = [0] * wanted
    rank = 0
    for b in range(count):
        one = fill[k, start + b]
        for p in range(wanted):
            found[p] = jnp.where((one == 1) & (rank == p), b, found[p])
        rank = rank + one
    return found


def block(at, size):
    return pl.ds(pl.multiple_of(at * size, size), size)


def pack_kernel(
    row_count, col_count, fill_in, green_in, factor_in, own_factor, mask, *refs
):
    greens, (fill, green, factor, sems) = refs[:row_count], refs[row_count:]
    copies = [
        pltpu.make_async_copy(source, target, sems.at[n])
        for n, (source, target) in enumerate(
            [(fill_in, fill), (factor_in, factor), (green_in, green)]
        )
    ]
    for one in copies:
        one.start()
    row_index = lax.axis_index("row")
    col_index = lax.axis_index("col")
    blocks = fill.shape[1]
    size = factor.shape[1] // blocks
    group = blocks // col_count
    half = group // 2
    chunk = blocks // row_count
    kept = chunk // 2
    copies[0].wait()
    chosen = [
        (
            places(fill, looked_up(ROW_MOVES[s], row_index), col_index * group, group, half),
            places(fill, looked_up(ROW_MOVES[s], row_index), row_index * chunk, chunk, kept),
        )
        for s in range(row_count)
    ]
    own = [
        part * chunk + b
        for part in range(row_count)
        for b in places(fill, row_index, part * chunk, chunk, kept)
    ]
    for p, r in enumerate(chosen[0][0]):
        for b in range(group):
            mask[p : p + 1, b * size : (b + 1) * size] = jnp.full(
                (1, size), jnp.where(r == b, 1.0, 0.0), jnp.float32
            )
    copies[1].wait()
    for p, b in enumerate(own):
        own_factor[:, p * size : (p + 1) * size] = factor[:, block(b, size)]
    copies[2].wait()
    for s, (rows, cols) in enumerate(chosen):
        for p, r in enumerate(rows):
            for q, c in enumerate(cols):
                greens[s][p * size : (p + 1) * size, q * size : (q + 1) * size] = green[
                    block(r, size), block(c, size)
                ]


def pack(green_top, factor_cols, fill_blocks):
    row_count = lax.axis_size("row")
    col_count = lax.axis_size("col")
    local_rows, order = factor_cols.shape
    blocks = fill_blocks.shape[1]
    size = order // blocks
    group = blocks // col_count
    half = group // 2
    kept = blocks // row_count // 2
    shapes = [
        pltpu.VMEM((local_rows, row_count * kept * size), jnp.bfloat16),
        pltpu.VMEM((half, group * size), jnp.float32),
    ] + [pltpu.VMEM((half * size, kept * size), jnp.bfloat16)] * row_count
    return pl.pallas_call(
        lambda *refs: pack_kernel(row_count, col_count, *refs),
        out_shape=shapes,
        in_specs=[pl.BlockSpec(memory_space=pltpu.HBM)] * 3,
        out_specs=[pl.BlockSpec(memory_space=pltpu.VMEM)] * len(shapes),
        scratch_shapes=[
            pltpu.SMEM(fill_blocks.shape, fill_blocks.dtype),
            pltpu.VMEM(green_top.shape, green_top.dtype),
            pltpu.VMEM(factor_cols.shape, factor_cols.dtype),
            pltpu.SemaphoreType.DMA((3,)),
        ],
        name="pack",
    )(fill_blocks, green_top, factor_cols)


def split(given, row_count, col_count):
    order = OPERANDS if (row_count, col_count) == (4, 4) else range(row_count + col_count)
    placed = dict(zip(order, given))
    return [placed[n] for n in range(col_count)], [
        placed[col_count + n] for n in range(row_count)
    ]


def solve_kernel(row_count, col_count, *refs):
    given, (solved, coded, factor) = refs[: row_count + col_count], refs[row_count + col_count :]
    factors, greens = split(given, row_count, col_count)
    row_index = lax.axis_index("row")
    col_index = lax.axis_index("col")
    local_rows = factors[0].shape[0]
    rows, width = greens[0].shape
    origins = [(0, 1, 2, 3)] + [(2, 3, 0, 1), (1, 0, 3, 2), (3, 2, 1, 0)]
    for origin, part in zip(origins, factors):
        place = sum(jnp.where(col_index == a, o, 0) for a, o in enumerate(origin))
        factor[block(place, local_rows), :] = part[...]
    total = jnp.zeros(solved.shape, jnp.float32)
    for s in range(row_count):
        total = total + lax.dot_general(
            factor[:, block(looked_up(sources(ROW_MOVES[s]), row_index), width)],
            greens[s][...],
            (((1,), (1,)), ((), ())),
            preferred_element_type=jnp.float32,
        )
    total = -total
    solved[...] = total
    pieces = []
    rest = total
    for _ in range(3):
        pieces.append(rest.astype(jnp.bfloat16))
        rest = rest - pieces[-1].astype(jnp.float32)
    own = factor[:, block(col_index, rows)]
    value = lax.dot_general(
        jnp.concatenate(pieces[::-1], axis=1),
        jnp.concatenate([own] * len(pieces), axis=1),
        (((1,), (1,)), ((), ())),
        preferred_element_type=jnp.float32,
    )
    largest = jnp.max(jnp.abs(value), axis=0, keepdims=True)
    exponent = jnp.floor(jnp.log2(jnp.maximum(largest, 2.0**-100)))
    scaled = jnp.round(value * jnp.exp2(14.0 - exponent))
    count = value.shape[0]
    coded[:count, :] = jnp.clip(scaled, -32767.0, 32767.0).astype(jnp.int32).astype(jnp.int16)
    coded[count:, :] = jnp.broadcast_to(
        exponent.astype(jnp.int32), (EXPONENT_ROWS, value.shape[1])
    ).astype(jnp.int16)


def solve(factors, greens):
    col_count, row_count = len(factors), len(greens)
    local_rows, columns = factors[0].shape
    count = col_count * local_rows
    return pl.pallas_call(
        lambda *refs: solve_kernel(row_count, col_count, *refs),
        out_shape=[
            pltpu.VMEM((count, greens[0].shape[0]), jnp.float32),
            pltpu.VMEM((count + EXPONENT_ROWS, count), jnp.int16),
        ],
        in_specs=[pl.BlockSpec(memory_space=pltpu.VMEM)] * (row_count + col_count),
        out_specs=[pl.BlockSpec(memory_space=pltpu.VMEM)] * 2,
        scratch_shapes=[pltpu.VMEM((count, columns), jnp.bfloat16)],
        compiler_params=pltpu.CompilerParams(vmem_limit_bytes=32 * 1024 * 1024),
        name="solve",
    )(*[(list(factors) + list(greens))[n] for n in (OPERANDS if (row_count, col_count) == (4, 4) else range(row_count + col_count))])


def finish_kernel(diag_inverse, *refs):
    codes, out = refs[:-1], refs[-1]
    count = diag_inverse.shape[0]
    sums = []
    for code in codes:
        exponent = code[count:, :].astype(jnp.int32).astype(jnp.float32)[:1]
        sums.append(code[:count, :].astype(jnp.int32).astype(jnp.float32) * jnp.exp2(exponent - 14.0))
    total = (sums[0] + sums[2]) + (sums[3] + sums[1])
    out[...] = diag_inverse[...] - total


def finish(diag_inverse, codes):
    return pl.pallas_call(
        finish_kernel,
        out_shape=jax.ShapeDtypeStruct(diag_inverse.shape, diag_inverse.dtype),
        in_specs=[pl.BlockSpec(memory_space=pltpu.VMEM)] * (1 + len(codes)),
        out_specs=pl.BlockSpec(memory_space=pltpu.VMEM),
        compiler_params=pltpu.CompilerParams(vmem_limit_bytes=32 * 1024 * 1024),
        name="finish",
    )(diag_inverse, *codes)


def per_device(green_top, factor_cols, fill_blocks, diag_inverse):
    row_count = lax.axis_size("row")
    col_count = lax.axis_size("col")
    blocks = fill_blocks.shape[1]
    chunk = blocks // row_count
    group = blocks // col_count
    if chunk % group or green_top.size > 1 << 20:
        return wide_device(green_top, factor_cols, fill_blocks, diag_inverse)
    half = group // 2
    size = factor_cols.shape[1] // blocks

    own_factor, mask, *greens = pack(green_top, factor_cols, fill_blocks)
    moves = {
        "b+": (1, 3, 0, 2),
        "b-": (2, 0, 3, 1),
        "z1": (1, 0, 3, 2),
        "z2": (2, 3, 0, 1),
        "z3": (3, 2, 1, 0),
    }

    def moved(value, name):
        return lax.ppermute(value, "col", list(enumerate(moves[name])))

    def crossed(value, m):
        return lax.ppermute(value, "row", list(enumerate(ROW_MOVES[m])))

    parts = {n: crossed(greens[m], m) for m, n in ((1, "c"), (2, "x"), (3, "xc"))}
    parts["z1"] = moved(own_factor, "z1")
    parts["z2"] = moved(own_factor, "z2")
    passed, *rest = lax.optimization_barrier((parts["z2"], *[parts[n] for n in []]))
    parts.update(zip([], rest))
    parts["fw"] = moved(passed, "z1")
    greens = [greens[0], parts["c"], parts["x"], parts["xc"]]
    factors = [own_factor] + [parts[n] for n in ['z2', 'z1', 'fw']]
    solved, code = solve(factors, greens)
    green_cols = None
    for p in range(half):
        term = mask[p : p + 1] * jnp.tile(solved[:, p * size : (p + 1) * size], (1, group))
        green_cols = term if green_cols is None else green_cols + term
    codes = [code] + [moved(code, name) for name in ['b-', 'z3', 'b+']]
    return (green_cols, finish(diag_inverse, codes))


def solution(mesh):
    placed = (
        P(("pole", "col"), "row"),
        P(("pole", "row", "col"), None),
        P(),
        P(("pole", "row"), None),
    )
    return jax.shard_map(
        per_device,
        mesh=mesh,
        in_specs=placed,
        out_specs=(P(("pole", "row"), "col"), P(("pole", "row"), None)),
        check_vma=False,
    )
```
